32 devices in a mesh: row: 4 (over z), col: 8 (over y, x, core).
Axes of the slice: x: 2, y: 2, z: 4, core: 2. Of those that a mesh axis runs over, the one named last changes fastest.
Arguments:
- hidden_acts: bfloat16 [1024, 26624], P('col', 'row'), may hold values from -0.1875 to 0.1875
- out_grad: bfloat16 [1024, 16384], P('row', 'col'), may hold values from -6 to 6
- down_weight: bfloat16 [26624, 16384], P('row', 'col'), may hold values from -0.046875 to 0.046875
Outputs:
- weight_grad: bfloat16 [26624, 16384], P('row', 'col')
- hidden_grad: bfloat16 [1024, 26624], P('col', 'row')
The draws below stay inside these ranges and needn't reach their ends.
All inputs are finite; a program needn't handle non-finite values.
Results may differ from the reference program's by a relative error of at most 0.02.
Values may be sent and summed in bfloat16 or wider, within the bound.
No kernel may reach another device: no remote copies, remote signals or barrier semaphores. Data moves between devices by JAX's collectives and lax.ppermute only.
A program may use at most 128 MiB of HBM per device.

```python
import jax
import jax.numpy as jnp

D = 16384
FF = 26624
TOKENS = 1024
N_COL = 8


def with_spikes(result, key, source, target, shards_of, factor):
    def block_of(axis_at):
        return (jnp.arange(result.shape[axis_at]) // (result.shape[axis_at] // shards_of)).reshape((-1,) + (1,) * (result.ndim - 1 - axis_at))

    near = jax.random.permutation(key, shards_of)[block_of(target)]
    second = (block_of(target) + shards_of // 2) % shards_of
    return jnp.where((block_of(source) == near) | (block_of(source) == second), factor * result, result)


def levels(own_key, dims, cuts, smallest, high):
    def one(position, shards_of):
        steps = jax.random.uniform(jax.random.fold_in(jax.random.fold_in(own_key, 6), position), (shards_of,), jnp.float32, smallest / len(cuts), high / len(cuts))
        return jnp.repeat(jnp.exp(steps), dims[position] // shards_of).reshape((-1,) + (1,) * (len(dims) - position - 1))

    factor_of = one(*cuts[0])
    for cut in cuts[1:]:
        factor_of = factor_of * one(*cut)
    return factor_of


def normal_values(key, shape, scale, most, split=(), held_as=jnp.bfloat16):
    result = scale * jax.random.normal(key, shape, jnp.float32)
    if split:
        result = result * levels(key, shape, split, -0.22, 0.18)
    return jnp.clip(result, -most, most).astype(held_as)


def gaussian_with(own_key, shape, scale, reach, cuts, heavy, kind=jnp.bfloat16):
    array = scale * jax.random.normal(own_key, shape, jnp.float32)
    if cuts:
        array = array * levels(own_key, shape, cuts, -0.22, 0.18)
    return jnp.clip(with_spikes(array, jax.random.fold_in(own_key, 3), *heavy), -reach, reach).astype(kind)


def setup_inputs(seed: int = 0) -> dict:
    keys = jax.random.split(jax.random.key(seed), 4)
    hidden_acts = normal_values(keys[0], (TOKENS, FF), (TOKENS ** -0.5), 0.1875, ((0, 8), (1, 4)))
    out_grad = gaussian_with(keys[1], (TOKENS, D), 1.0, 6.0, ((0, 4), (1, 8)), (1, 0, 8, 2.0))
    down_weight = normal_values(keys[2], (FF, D), D ** -0.5, 0.046875, ((0, 4), (1, 8)))
    return dict(hidden_acts=hidden_acts, out_grad=out_grad, down_weight=down_weight)


def reference(hidden_acts, out_grad, down_weight):
    weight_grad = jnp.dot(hidden_acts.T, out_grad, preferred_element_type=jnp.float32).astype(jnp.bfloat16)
    width = D // N_COL
    total = jnp.zeros((out_grad.shape[0], down_weight.shape[0]), jnp.float32)
    for group in range(N_COL):
        grad_part = out_grad[:, group * width:(group + 1) * width]
        weight_part = down_weight[:, group * width:(group + 1) * width]
        partial_grad = jnp.dot(grad_part, weight_part.T, preferred_element_type=jnp.float32).astype(jnp.bfloat16)
        total = total + partial_grad.astype(jnp.float32)
    return weight_grad, total.astype(jnp.bfloat16)
```

```python
import functools

import jax
import jax.numpy as jnp
from jax import lax
from jax.experimental import pallas as pl
from jax.experimental.pallas import tpu as pltpu
from jax.sharding import PartitionSpec as P

F32, BF16 = jnp.float32, jnp.bfloat16
ANYWHERE = pl.BlockSpec(memory_space=pl.ANY)
PARAMS = pltpu.CompilerParams(vmem_limit_bytes=58 * 1024 * 1024)


def halving_order(bits):
    if not bits:
        return [0]
    keep = halving_order(bits[1:])
    return [o ^ bits[0] for o in keep] + keep


def flip(x, bit, n):
    return lax.ppermute(x, "col", [(i, i ^ bit) for i in range(n)])


def partial_kernel(order, c, me_ref, g_ref, w_ref, *refs):
    send_ref, keep_ref, rel = refs[-3:]
    half = len(order) // 2

    @pl.when(pl.program_id(0) == 0)
    def _():
        for p, j in enumerate(order):
            start = pl.multiple_of((me_ref[0] ^ j) * c, c)
            rel[pl.ds(p * c, c), :] = g_ref[pl.ds(start, c), :]

    res = lax.dot_general(
        rel[...], w_ref[...], (((1,), (1,)), ((), ())), preferred_element_type=F32
    ).astype(BF16)
    res = res.reshape(2 * half, c, res.shape[-1])
    send_ref[...] = res[:half]
    keep_ref[...] = res[half:]


def partial_sums(me, grads, weight, order, c, tile, first, count, after):
    n, depth = len(order), grads.shape[1]
    out = jax.ShapeDtypeStruct((n // 2, c, count * tile), BF16)
    out_spec = pl.BlockSpec((n // 2, c, tile), lambda i, s: (0, 0, i))
    return pl.pallas_call(
        functools.partial(partial_kernel, order, c),
        out_shape=(out, out),
        grid_spec=pltpu.PrefetchScalarGridSpec(
            num_scalar_prefetch=1,
            grid=(count,),
            in_specs=[
                pl.BlockSpec((n * c, depth), lambda i, s: (0, 0)),
                pl.BlockSpec((tile, depth), lambda i, s: (first + i, 0)),
            ]
            + [ANYWHERE] * len(after),
            out_specs=(out_spec, out_spec),
            scratch_shapes=[pltpu.VMEM((n * c, depth), BF16)],
        ),
        compiler_params=PARAMS,
        cost_estimate=pl.CostEstimate(
            flops=2 * n * c * depth * count * tile,
            bytes_accessed=2 * (n * c * depth + count * tile * depth + n * c * count * tile),
            transcendentals=0,
        ),
        name="partial_sums",
    )(me, grads, weight, *after)


def weight_kernel(places, chunks, n, me_ref, *refs):
    acts_refs, refs = refs[: len(places)], refs[len(places):]
    grads_refs, out_ref, acts = refs[: len(chunks)], refs[-2], refs[-1]
    for (j, begin), ref in zip(places, acts_refs):
        for at, c in chunks:
            if begin <= at and at + c <= begin + ref.shape[0]:
                start = pl.multiple_of(at * n + (me_ref[0] ^ j) * c, c)
                acts[pl.ds(start, c), :] = ref[pl.ds(at - begin, c), :]
    total = None
    for (at, c), ref in zip(chunks, grads_refs):
        term = lax.dot_general(
            acts[pl.ds(at * n, c * n), :], ref[...],
            (((0,), (0,)), ((), ())), preferred_element_type=F32,
        )
        total = term if total is None else total + term
    out_ref[...] = total.astype(BF16)


def weight_rows(me, pieces, grads, chunks, n, before, shape, tile, first, count, after):
    places = [place for place, _ in pieces]
    rows, width = sum(g.shape[0] for g in grads), shape[1]
    in_specs = [pl.BlockSpec((a.shape[0], tile), lambda i, s: (0, first + i)) for _, a in pieces]
    in_specs += [
        pl.BlockSpec(g.shape, lambda i, s: (0, 0), pipeline_mode=pl.Buffered(1)) for g in grads
    ]
    args = [a for _, a in pieces] + list(grads) + list(after)
    in_specs += [ANYWHERE] * len(after)
    aliases = {}
    if before is not None:
        in_specs.append(ANYWHERE)
        args.append(before)
        aliases = {len(args): 0}
    return pl.pallas_call(
        functools.partial(weight_kernel, places, chunks, n),
        out_shape=jax.ShapeDtypeStruct(shape, BF16),
        grid_spec=pltpu.PrefetchScalarGridSpec(
            num_scalar_prefetch=1,
            grid=(count,),
            in_specs=in_specs,
            out_specs=pl.BlockSpec((tile, width), lambda i, s: (first + i, 0)),
            scratch_shapes=[pltpu.VMEM((rows, tile), BF16)],
        ),
        input_output_aliases=aliases,
        compiler_params=PARAMS,
        cost_estimate=pl.CostEstimate(
            flops=2 * rows * width * count * tile,
            bytes_accessed=2 * (rows * width + (rows + width) * count * tile),
            transcendentals=0,
        ),
        name="weight_rows",
    )(me, *args)


def sums_kernel(sizes, n_final, *refs):
    outs = refs[-len(sizes) + n_final - 1:] if n_final else refs[-len(sizes):]
    at, column = 0, 0
    for job, size in enumerate(sizes):
        total = refs[at][...].astype(F32)
        for ref in refs[at + 1 : at + size]:
            total = total + ref[...].astype(F32)
        at += size
        if job < len(sizes) - n_final:
            outs[job][...] = total.astype(BF16)
        else:
            width = total.shape[-1]
            outs[-1][:, pl.ds(column, width)] = total[0].astype(BF16)
            column += width


def sums(jobs, after, final=None, shape=None, before=None):
    final, at = final or ([], 0)
    everything = jobs + final
    heights = [job[0][0][0].shape[1] for job in everything]
    steps = min(4, min(heights) // 16)
    in_specs, args, out_specs, out_shape = [], [], [], []
    for job, (terms, size) in enumerate(everything):
        _, c, f = terms[0][0].shape
        for array, first in terms:
            in_specs.append(
                pl.BlockSpec((size, c // steps, f), lambda i, b=first // size: (b, i, 0))
            )
            args.append(array)
        if job < len(jobs):
            out_specs.append(pl.BlockSpec((size, c // steps, f), lambda i: (0, i, 0)))
            out_shape.append(jax.ShapeDtypeStruct((size, c, f), BF16))
    args += after
    in_specs += [ANYWHERE] * len(after)
    aliases = {}
    if final:
        height = heights[-1] // steps
        out_specs.append(pl.BlockSpec((height, shape[1]), lambda i: (at // height + i, 0)))
        out_shape.append(jax.ShapeDtypeStruct(shape, BF16))
        if before is not None:
            aliases = {len(args): len(jobs)}
            args.append(before)
            in_specs.append(ANYWHERE)
    bytes_accessed = sum(
        2 * (len(terms) + 1) * size * terms[0][0].shape[1] * terms[0][0].shape[2]
        for terms, size in everything
    )
    return pl.pallas_call(
        functools.partial(sums_kernel, [len(terms) for terms, _ in everything], len(final)),
        out_shape=out_shape,
        grid=(steps,),
        in_specs=in_specs,
        out_specs=out_specs,
        input_output_aliases=aliases,
        compiler_params=PARAMS,
        cost_estimate=pl.CostEstimate(
            flops=bytes_accessed, bytes_accessed=bytes_accessed, transcendentals=0
        ),
        name="sums",
    )(*args)


class Halving:
    def __init__(self, send, keep, bits, n):
        self.bits, self.n = list(bits), n
        self.kept, self.offset = keep.shape[0], 0
        self.terms = [[keep, 0]]
        self.take(send)

    def take(self, out):
        self.terms = self.terms + [[flip(out, self.bits.pop(0), self.n), 0]]

    def job(self):
        size = self.kept // 2 if self.bits else 1
        self.kept = size
        job = ([(array, first) for array, first in self.terms], size)
        self.terms = [[array, first + size] for array, first in self.terms]
        return job


def per_device(n_row, n_col, hidden_acts, out_grad, down_weight):
    tokens, units = hidden_acts.shape
    features = out_grad.shape[1]
    owners = n_col // n_row
    bits = [1 << b for b in range(n_col.bit_length() - 1)]
    sizes = [tokens // 2] + ([tokens // 4] * 2 if tokens >= 64 else [tokens // 2])
    chunks = [(sum(sizes[:k]), c) for k, c in enumerate(sizes)]
    tile = 128 * max(d for d in (1, 2, 4) if units % (128 * d) == 0)
    tiles = units // tile
    me = lax.axis_index("col").astype(jnp.int32).reshape(1)

    by_owner = out_grad.reshape(owners, tokens, features)
    grads = [
        lax.all_gather(by_owner[:, at : at + c], "row").reshape(n_col * c, features)
        for at, c in chunks
    ]

    half = tokens // 2
    whole = {0: hidden_acts}
    for bit in bits[1:]:
        whole[bit] = flip(hidden_acts, bit, n_col)
    first_hop = [whole[bit] for bit in bits[1:]]
    for j in list(whole):
        whole[j ^ 1] = flip(whole[j], 1, n_col)
    pieces = [((j, 0), a) for j, a in whole.items()]
    for h, far in enumerate((bits[1:], bits[:0:-1])):
        held = {}
        for bit in far:
            for j in list(held):
                held[j ^ bit] = flip(held[j], bit, n_col)
            held[bit] = whole[bit][h * half : (h + 1) * half]
        for j, a in held.items():
            if j not in whole:
                pieces += [((j, h * half), a), ((j ^ 1, h * half), flip(a, 1, n_col))]

    split = (tiles + 1) // 2
    ranges = [(0, split, bits), (split, tiles - split, bits[:1] + bits[:0:-1])]

    def start(k, after):
        at, c = chunks[k]
        parts = []
        for first, count, order in ranges:
            send, keep = partial_sums(
                me, grads[k], down_weight, halving_order(order), c, tile, first, count, after
            )
            parts.append(Halving(send, keep, order, n_col))
            after = [send]
        return parts, after

    cuts = [round(tiles * f / 13) for f in (0, 4, 6, 10, 13)]
    weight_grad, hidden_grad = None, None

    def work(w, after):
        nonlocal weight_grad
        weight_grad = weight_rows(
            me, pieces, grads, chunks, n_col, weight_grad, (units, features), tile,
            cuts[w], cuts[w + 1] - cuts[w], after,
        )
        return [weight_grad]

    def advance(parts, after):
        nonlocal hidden_grad
        going = [p for chunk in parts for p in chunk[1] if p.bits]
        ended = [chunk for chunk in parts if not chunk[1][0].bits]
        assert len(ended) < 2
        final = ([p.job() for p in ended[0][1]], chunks[ended[0][0]][0]) if ended else None
        outs = sums([p.job() for p in going], after, final, (tokens, units), hidden_grad)
        for p, out in zip(going, outs):
            p.take(out)
        if ended:
            hidden_grad = outs[-1]
        return [outs[0]]

    after, parts, w = first_hop, [], 0
    for k in range(len(chunks)):
        if k == len(chunks) - 1:
            after, w = work(0, after), 1
        new, after = start(k, after)
        parts.append((k, new))
        if k == len(chunks) - 1:
            after, w = work(1, after), 2
        after = advance(parts, after)
        parts = [p for p in parts if p[1][0].terms[0][1] < n_col // 2]
    while parts:
        if w < len(cuts) - 1:
            after, w = work(w, after), w + 1
        after = advance(parts, after)
        parts = [p for p in parts if p[1][0].terms[0][1] < n_col // 2]
    return weight_grad, hidden_grad


def solution(mesh):
    in_specs = (P("col", "row"), P("row", "col"), P("row", "col"))
    out_specs = (P("row", "col"), P("col", "row"))
    return jax.shard_map(
        functools.partial(per_device, mesh.shape["row"], mesh.shape["col"]),
        mesh=mesh, in_specs=in_specs, out_specs=out_specs, check_vma=False,
    )
```

```python
import functools

import jax
import jax.numpy as jnp
from jax import lax
from jax.experimental import pallas as pl
from jax.experimental.pallas import tpu as pltpu
from jax.sharding import PartitionSpec as P

F32, BF16 = jnp.float32, jnp.bfloat16
ANYWHERE = pl.BlockSpec(memory_space=pl.ANY)
PARAMS = pltpu.CompilerParams(vmem_limit_bytes=58 * 1024 * 1024)


def cost(flops, values):
    return pl.CostEstimate(flops=flops, bytes_accessed=2 * values, transcendentals=0)


def halving_order(bits):
    if not bits:
        return [0]
    keep = halving_order(bits[1:])
    return [o ^ bits[0] for o in keep] + keep


def flip(x, bits, n):
    return lax.ppermute(x, "col", [(i, i ^ bits[i & 1]) for i in range(n)])


def near_shift(x, s, n):
    pairs = [(i, (i + s) % n) for i in range(n)]
    return lax.ppermute(x, "row", [(i, j) for i, j in pairs if abs(i - j) <= n // 2])


def far_shift(x, e, n):
    half = n // 2
    up = [(i, i + e) for i in range(half, n - e)]
    down = [(i, i - e) for i in range(e, half)]
    return lax.ppermute(x, "row", up + down)


def assemble_kernel(n_row, orders, c, where_ref, own_ref, *refs):
    half = n_row // 2
    near, far = refs[: n_row - 1], refs[n_row - 1 : n_row + half - 2]
    grads_ref, turned_ref, rel = refs[-3:]
    me, row = where_ref[0], where_ref[1]
    rows = own_ref.shape[0]

    def put(s, ref):
        start = pl.multiple_of(lax.rem(row - s + n_row, n_row) * rows, rows)
        grads_ref[pl.ds(start, rows), :] = ref[...]

    put(0, own_ref)
    for s in range(1, n_row):
        if s == half:
            put(s, near[s - 1])
            continue
        came_far = (row < s) if s < half else (row >= s)
        pl.when(came_far)(functools.partial(put, s, far[abs(s - half) - 1]))
        pl.when(jnp.logical_not(came_far))(functools.partial(put, s, near[s - 1]))
    for p, (j0, j1) in enumerate(zip(*orders)):
        start = pl.multiple_of((me ^ jnp.where(me & 1, j1, j0)) * c, c)
        rel[pl.ds(p * c, c), :] = grads_ref[pl.ds(start, c), :]
    turned_ref[...] = rel[...].T


def assemble(where, own, near, far, orders, c, after):
    n_row, depth, rows = len(near) + 1, own.shape[1], len(orders[0]) * c
    steps = 2
    part = pl.BlockSpec((own.shape[0], depth // steps), lambda i, s: (0, i))
    arrays = [own, *near, *far]
    return pl.pallas_call(
        functools.partial(assemble_kernel, n_row, orders, c),
        out_shape=(
            jax.ShapeDtypeStruct((rows, depth), BF16),
            jax.ShapeDtypeStruct((depth, rows), BF16),
        ),
        grid_spec=pltpu.PrefetchScalarGridSpec(
            num_scalar_prefetch=1,
            grid=(steps,),
            in_specs=[part] * len(arrays) + [ANYWHERE] * len(after),
            out_specs=(
                pl.BlockSpec((rows, depth // steps), lambda i, s: (0, i)),
                pl.BlockSpec((depth // steps, rows), lambda i, s: (i, 0)),
            ),
            scratch_shapes=[pltpu.VMEM((rows, depth // steps), BF16)],
        ),
        compiler_params=PARAMS,
        cost_estimate=cost(0, 3 * rows * depth),
        name="assemble",
    )(where, *arrays, *after)


def partial_kernel(w_ref, g_ref, *refs):
    send_ref, keep_ref = refs[-2:]
    res = jnp.dot(w_ref[...], g_ref[...], preferred_element_type=F32).astype(BF16).T
    rows = res.shape[0] // 2
    send_ref[...] = res[:rows].reshape(send_ref.shape)
    keep_ref[...] = res[rows:].reshape(keep_ref.shape)


def partial_sums(turned, weight, n, c, tile, first, count, after):
    depth = weight.shape[1]
    out = jax.ShapeDtypeStruct((n // 2, c, count * tile), BF16)
    out_spec = pl.BlockSpec((n // 2, c, tile), lambda i: (0, 0, i))
    return pl.pallas_call(
        partial_kernel,
        out_shape=(out, out),
        grid=(count,),
        in_specs=[
            pl.BlockSpec((tile, depth), lambda i: (first + i, 0)),
            pl.BlockSpec((depth, n * c), lambda i: (0, 0), pipeline_mode=pl.Buffered(1)),
        ]
        + [ANYWHERE] * len(after),
        out_specs=(out_spec, out_spec),
        compiler_params=PARAMS,
        cost_estimate=cost(
            2 * n * c * depth * count * tile,
            n * c * depth + count * tile * depth + n * c * count * tile,
        ),
        name="partial_sums",
    )(weight, turned, *after)


def weight_kernel(places, chunks, n, where_ref, *refs):
    acts_refs, refs = refs[: len(places)], refs[len(places):]
    grads_refs, out_ref, acts = refs[: len(chunks)], refs[-2], refs[-1]
    me = where_ref[0]
    for (j0, j1), ref in zip(places, acts_refs):
        owner = me ^ jnp.where(me & 1, j1, j0)
        for at, c in chunks:
            start = pl.multiple_of(at * n + owner * c, c)
            acts[pl.ds(start, c), :] = ref[pl.ds(at, c), :]
    total = None
    for (at, c), ref in zip(chunks, grads_refs):
        term = lax.dot_general(
            acts[pl.ds(at * n, c * n), :], ref[...],
            (((0,), (0,)), ((), ())), preferred_element_type=F32,
        )
        total = term if total is None else total + term
    out_ref[...] = total.astype(BF16)


def weight_rows(where, pieces, grads, chunks, n, before, shape, tile, first, count, after):
    places = [place for place, _ in pieces]
    rows, width = sum(g.shape[0] for g in grads), shape[1]
    in_specs = [pl.BlockSpec((a.shape[0], tile), lambda i, s: (0, first + i)) for _, a in pieces]
    in_specs += [
        pl.BlockSpec(g.shape, lambda i, s: (0, 0), pipeline_mode=pl.Buffered(1)) for g in grads
    ]
    args = [a for _, a in pieces] + list(grads) + list(after)
    in_specs += [ANYWHERE] * len(after)
    aliases = {}
    if before is not None:
        in_specs.append(ANYWHERE)
        args.append(before)
        aliases = {len(args): 0}
    return pl.pallas_call(
        functools.partial(weight_kernel, places, chunks, n),
        out_shape=jax.ShapeDtypeStruct(shape, BF16),
        grid_spec=pltpu.PrefetchScalarGridSpec(
            num_scalar_prefetch=1,
            grid=(count,),
            in_specs=in_specs,
            out_specs=pl.BlockSpec((tile, width), lambda i, s: (first + i, 0)),
            scratch_shapes=[pltpu.VMEM((rows, tile), BF16)],
        ),
        input_output_aliases=aliases,
        compiler_params=PARAMS,
        cost_estimate=cost(
            2 * rows * width * count * tile, rows * width + (rows + width) * count * tile
        ),
        name="weight_rows",
    )(where, *args)


def sums_kernel(jobs, n_final, *refs):
    n_out = len(jobs) - n_final + (n_final > 0)
    outs, base = refs[-n_out:], 0
    at = 0
    for job, (width, cuts, spans) in enumerate(jobs):
        for lo, hi in zip(cuts, cuts[1:]):
            total = None
            for (begin, end), ref in zip(spans, refs[at : at + len(spans)]):
                if begin <= lo and hi <= end:
                    term = ref[:, :, lo - begin : hi - begin].astype(F32)
                    total = term if total is None else total + term
            if job < n_out - (n_final > 0):
                outs[job][:, :, lo:hi] = total.astype(BF16)
            else:
                outs[-1][:, base + lo : base + hi] = total[0].astype(BF16)
        if job >= len(jobs) - n_final:
            base += width
        at += len(spans)


def sums(going, ended, at, shape, before, after):
    parts = going + ended
    jobs = [part.job() for part in parts]
    steps = min(2, min(part.c for part in parts) // 16)
    in_specs, args, out_specs, out_shape, values = [], [], [], [], 0
    for part, (terms, size) in zip(parts, jobs):
        for array, first, _ in terms:
            in_specs.append(
                pl.BlockSpec(
                    (size, part.c // steps, array.shape[2]),
                    lambda i, b=first // size: (b, i, 0),
                )
            )
            args.append(array)
        values += (len(terms) + 1) * size * part.c * part.width
        if part in going:
            out_specs.append(pl.BlockSpec((size, part.c // steps, part.width), lambda i: (0, i, 0)))
            out_shape.append(jax.ShapeDtypeStruct((size, part.c, part.width), BF16))
    args += after
    in_specs += [ANYWHERE] * len(after)
    aliases = {}
    if ended:
        height = ended[0].c // steps
        out_specs.append(pl.BlockSpec((height, shape[1]), lambda i: (at // height + i, 0)))
        out_shape.append(jax.ShapeDtypeStruct(shape, BF16))
        if before is not None:
            aliases = {len(args): len(going)}
            args.append(before)
            in_specs.append(ANYWHERE)
    layout = [
        (part.width, part.cuts, [span for _, _, span in terms])
        for part, (terms, _) in zip(parts, jobs)
    ]
    outs = pl.pallas_call(
        functools.partial(sums_kernel, layout, len(ended)),
        out_shape=out_shape,
        grid=(steps,),
        in_specs=in_specs,
        out_specs=out_specs,
        input_output_aliases=aliases,
        compiler_params=PARAMS,
        cost_estimate=cost(values, values),
        name="sums",
    )(*args)
    for part, out in zip(going, outs):
        part.take(out)
    return outs[-1] if ended else before, [outs[0]]


class Halving:
    def __init__(self, sends, keeps, levels, n):
        self.levels, self.n = list(levels), n
        self.half, self.c = keeps[0].shape[:2]
        self.cuts = [0]
        for keep in keeps:
            self.cuts.append(self.cuts[-1] + keep.shape[2])
        self.width = self.cuts[-1]
        spans = list(zip(self.cuts, self.cuts[1:]))
        bits = self.levels.pop(0)
        self.terms = [[keep, 0, span] for keep, span in zip(keeps, spans)]
        self.terms += [[flip(send, bits, n), 0, span] for send, span in zip(sends, spans)]

    def take(self, out):
        self.terms.append([flip(out, self.levels.pop(0), self.n), 0, (0, self.width)])

    def job(self):
        size = self.half = self.half // 2 if self.levels else 1
        job = ([tuple(term) for term in self.terms], size)
        self.terms = [[array, first + size, span] for array, first, span in self.terms]
        return job


def hold_kernel(*refs):
    refs[-1][...] = jnp.zeros_like(refs[-1])


def hold(after):
    return pl.pallas_call(
        hold_kernel,
        out_shape=jax.ShapeDtypeStruct((8, 128), F32),
        grid=(1,),
        in_specs=[ANYWHERE] * len(after),
        out_specs=pl.BlockSpec((8, 128), lambda i: (0, 0)),
        compiler_params=PARAMS,
        cost_estimate=cost(50 * 10**9, 8 * 128),
        name="hold",
    )(*after)


def per_device(n_row, n_col, hidden_acts, out_grad, down_weight):
    tokens, units = hidden_acts.shape
    features = out_grad.shape[1]
    owners = n_col // n_row
    further = [1 << b for b in range(1, n_col.bit_length() - 1)]
    levels = [(1, 1), *zip(further, further[::-1])]
    kept = [halving_order([bits[h] for bits in levels[1:]]) for h in (0, 1)]
    orders = [[o ^ 1 for o in kept[1 - h]] + kept[h] for h in (0, 1)]
    c = tokens // 2
    chunks = [(0, c), (c, c)]
    tile = 128 * max(d for d in (1, 2, 4) if units % (128 * d) == 0)
    tiles = units // tile
    cut = (tiles + 1) // 2
    col, row = lax.axis_index("col"), lax.axis_index("row")
    where = jnp.stack([col, row]).astype(jnp.int32)

    whole = {bit: flip(hidden_acts, (bit, bit), n_col) for bit in further}

    by_owner = out_grad.reshape(owners, tokens, features)
    own = [by_owner[:, at : at + c].reshape(owners * c, features) for at, c in chunks]

    def near_blocks(x):
        return [near_shift(x, s, n_row) for s in range(1, n_row)]

    def far_blocks(near):
        return [far_shift(near[n_row // 2 - 1], e, n_row) for e in range(1, n_row // 2)]

    near0 = near_blocks(own[0])
    *near0, own[1] = lax.optimization_barrier((*near0, own[1]))
    far0 = far_blocks(near0)
    near1 = near_blocks(own[1])
    grads0, turned0 = assemble(where, own[0], near0, far0, orders, c, list(whole.values()))

    corners = []
    for t, bits in enumerate(levels[1:]):
        passed = [((j0 ^ bits[0], j1 ^ bits[1]), flip(a, bits, n_col)) for (j0, j1), a in corners]
        if t < len(further) - 1:
            mine = jnp.where(col & 1, whole[bits[1]], whole[bits[0]])
            corners = corners + passed + [(bits, mine)]
        else:
            corners = corners + passed
    corners = [((j0, j1), a) for (j0, j1), a in corners if j0 not in whole]

    def partials(turned, first, count, after):
        send, keep = partial_sums(turned, down_weight, n_col, c, tile, first, count, after)
        return send, keep, [send]

    send, keep, after = partials(turned0, 0, tiles, [])
    zero = Halving([send], [keep], levels, n_col)

    *near1, tied = lax.optimization_barrier((*near1, after[0]))
    far1 = far_blocks(near1)
    pieces = [((0, 0), hidden_acts)] + [((j, j), a) for j, a in whole.items()] + corners
    pieces += [((j1 ^ 1, j0 ^ 1), flip(a, (1, 1), n_col)) for (j0, j1), a in pieces]

    hidden_grad, weight_grad, done = None, None, 0

    def advance(going, ended, at, after):
        nonlocal hidden_grad
        hidden_grad, after = sums(going, ended, at, (tokens, units), hidden_grad, after)
        return after

    def work(count, after):
        nonlocal weight_grad, done
        count = min(tiles - done, count)
        if count:
            weight_grad = weight_rows(
                where, pieces, grads, chunks, n_col, weight_grad, (units, features), tile,
                done, count, after,
            )
            done += count
        return [weight_grad]

    after = [hold([tied] + near1 + [a for _, a in corners])]
    after = advance([zero], [], 0, after)
    exchanged = [a for _, a in pieces[n_col // 2 :]]
    grads1, turned1 = assemble(where, own[1], near1, far1, orders, c, after + exchanged[:1])
    grads = [grads0, grads1]
    send_a, keep_a, after = partials(turned1, 0, cut, after)
    a1 = Halving([send_a], [keep_a], levels, n_col)
    send_b, keep_b, after = partials(turned1, cut, tiles - cut, after)
    b1 = Halving([send_b], [keep_b], levels, n_col)
    after = advance([zero, a1], [], 0, after)
    after = work(2, after)
    after = advance([b1], [], 0, after)
    parts, steps = [zero, a1, b1], len(levels) - 1
    for step in range(steps):
        after = work(-(-(tiles - done) // (steps - step)), after)
        going, ended = [p for p in parts if p.levels], [p for p in parts if not p.levels]
        after = advance(going, ended, 0 if zero in ended else c, after)
        parts = going
    return weight_grad, hidden_grad


def solution(mesh):
    in_specs = (P("col", "row"), P("row", "col"), P("row", "col"))
    out_specs = (P("row", "col"), P("col", "row"))
    return jax.shard_map(
        functools.partial(per_device, mesh.shape["row"], mesh.shape["col"]),
        mesh=mesh, in_specs=in_specs, out_specs=out_specs, check_vma=False,
    )
```

```python
import functools

import jax
import jax.numpy as jnp
from jax import lax
from jax.experimental import pallas as pl
from jax.experimental.pallas import tpu as pltpu
from jax.sharding import PartitionSpec as P

F32, BF16 = jnp.float32, jnp.bfloat16
ANYWHERE = pl.BlockSpec(memory_space=pl.ANY)
PARAMS = pltpu.CompilerParams(vmem_limit_bytes=58 * 1024 * 1024)


def cost(flops, values):
    return pl.CostEstimate(flops=flops, bytes_accessed=2 * values, transcendentals=0)


def once(shape, index):
    return pl.BlockSpec(shape, lambda *_: index, pipeline_mode=pl.Buffered(1))


def halving_order(bits):
    if not bits:
        return [0]
    keep = halving_order(bits[1:])
    return [o ^ bits[0] for o in keep] + keep


def flip(x, bits, n):
    return lax.ppermute(x, "col", [(i, i ^ bits[i & 1]) for i in range(n)])


def near_shift(x, s, n):
    pairs = [(i, (i + s) % n) for i in range(n)]
    return lax.ppermute(x, "row", [(i, j) for i, j in pairs if abs(i - j) <= n // 2])


def far_shift(x, e, n):
    half = n // 2
    up = [(i, i + e) for i in range(half, n - e)]
    down = [(i, i - e) for i in range(e, half)]
    return lax.ppermute(x, "row", up + down)


def slot_of(row, owner, n_row):
    return lax.rem(row - owner // 2 - 1 + n_row, n_row)


def turn_kernel(c, where_ref, own_ref, w_ref, turned_ref, *refs):
    outs, mine = refs[:-1], refs[-1]
    core = where_ref[0] & 1

    @pl.when(pl.program_id(0) == 0)
    def _():
        for p in range(4):
            h = core if p % 2 else 1 - core
            mine[pl.ds(p * c, c), :] = own_ref[h, pl.ds(p // 2 * c, c), :]

    turned = w_ref[...].T
    turned_ref[0] = turned
    res = jnp.dot(mine[...], turned, preferred_element_type=F32).astype(BF16)
    for p, ref in enumerate(outs):
        ref[0] = res[p * c : (p + 1) * c]


def turn_weights(where, own, weight, c, n_row, tile):
    units, depth = weight.shape
    tiles = units // tile
    part = jax.ShapeDtypeStruct((n_row, c, units), BF16)
    part_spec = pl.BlockSpec((1, c, tile), lambda i, s: (n_row - 1, 0, i))
    return pl.pallas_call(
        functools.partial(turn_kernel, c),
        out_shape=(jax.ShapeDtypeStruct((tiles, depth, tile), BF16),) + (part,) * 4,
        grid_spec=pltpu.PrefetchScalarGridSpec(
            num_scalar_prefetch=1,
            grid=(tiles,),
            in_specs=[once(own.shape, (0, 0, 0)), pl.BlockSpec((tile, depth), lambda i, s: (i, 0))],
            out_specs=(pl.BlockSpec((1, depth, tile), lambda i, s: (i, 0, 0)),) + (part_spec,) * 4,
            scratch_shapes=[pltpu.VMEM((4 * c, depth), BF16)],
        ),
        compiler_params=PARAMS,
        cost_estimate=cost(8 * c * depth * units, 2 * units * depth + 4 * c * units),
        name="turn_weights",
    )(where, own, weight)


def partial_kernel(n_row, c, where_ref, w_ref, *refs):
    half = n_row // 2
    near, far = refs[: n_row - 1], refs[n_row - 1 : n_row + half - 2]
    send_ref, keep_ref, rows_ref, lhs = refs[-4:]
    core, row = where_ref[0] & 1, where_ref[1]
    count = (n_row - 1) * c

    def put(s, ref):
        lhs[pl.ds((s - 1) * c, c), :] = ref[1 - core]
        lhs[pl.ds(count + (s - 1) * c, c), :] = ref[core]

    @pl.when(pl.program_id(0) == 0)
    def _():
        for s in range(1, n_row):
            if s == half:
                put(s, near[s - 1])
                continue
            came_far = (row < s) if s < half else (row >= s)
            pl.when(came_far)(functools.partial(put, s, far[abs(s - half) - 1]))
            pl.when(jnp.logical_not(came_far))(functools.partial(put, s, near[s - 1]))
        rows_ref[...] = lhs[...]

    res = jnp.dot(lhs[...], w_ref[0], preferred_element_type=F32).astype(BF16)
    send_ref[...] = res[:count].reshape(send_ref.shape)
    keep_ref[...] = res[count:].reshape(keep_ref.shape)


def partial_sums(where, turned, near, far, send, keep, k, after):
    n_row, c, units = send.shape
    tiles, depth, tile = turned.shape
    count = 2 * (n_row - 1) * c
    blocks = near + far
    in_specs = [pl.BlockSpec((1, depth, tile), lambda i, s: (i, 0, 0))]
    in_specs += [once((2, c, depth), (0, k if a.shape[1] > c else 0, 0)) for a in blocks]
    in_specs += [ANYWHERE] * (2 + len(after))
    part = jax.ShapeDtypeStruct(send.shape, BF16)
    part_spec = pl.BlockSpec((n_row - 1, c, tile), lambda i, s: (0, 0, i))
    return pl.pallas_call(
        functools.partial(partial_kernel, n_row, c),
        out_shape=(part, part, jax.ShapeDtypeStruct((count, depth), BF16)),
        grid_spec=pltpu.PrefetchScalarGridSpec(
            num_scalar_prefetch=1,
            grid=(tiles,),
            in_specs=in_specs,
            out_specs=(part_spec, part_spec, pl.BlockSpec((count, depth), lambda i, s: (0, 0))),
            scratch_shapes=[pltpu.VMEM((count, depth), BF16)],
        ),
        input_output_aliases={2 + len(blocks): 0, 3 + len(blocks): 1},
        compiler_params=PARAMS,
        cost_estimate=cost(
            2 * count * depth * units, 2 * count * depth + units * depth + count * units
        ),
        name="partial_sums",
    )(where, turned, *blocks, send, keep, *after)


def weight_kernel(places, n_row, c, where_ref, *refs):
    acts_refs, refs = refs[: len(places)], refs[len(places):]
    own_ref, grads_refs, out_ref, acts = refs[0], refs[1:3], refs[-2], refs[-1]
    me, row = where_ref[0], where_ref[1]
    core, tokens, count = me & 1, 2 * c, 2 * (n_row - 1) * c
    for (j0, j1), ref in zip(places, acts_refs):
        owner = me ^ jnp.where(core == 1, j1, j0)
        h = owner & 1
        slot = slot_of(row, owner, n_row) + jnp.where(h == core, n_row - 1, 0)
        for k in range(2):
            start = jnp.where(
                owner // 2 == row, 2 * count + h * tokens + k * c, k * count + slot * c
            )
            acts[pl.ds(pl.multiple_of(start, c), c), :] = ref[pl.ds(k * c, c), :]
    terms = [(0, grads_refs[0][...]), (count, grads_refs[1][...])]
    terms.append((2 * count, own_ref[...].reshape(2 * tokens, own_ref.shape[2])))
    total = None
    for start, rows in terms:
        term = lax.dot_general(
            acts[pl.ds(start, rows.shape[0]), :], rows,
            (((0,), (0,)), ((), ())), preferred_element_type=F32,
        )
        total = term if total is None else total + term
    out_ref[...] = total.astype(BF16)


def weight_rows(where, pieces, own, grads, before, shape, n_row, c, tile, first, count, after):
    places = [place for place, _ in pieces]
    rows, width = 2 * n_row * 2 * c, shape[1]
    in_specs = [pl.BlockSpec((a.shape[0], tile), lambda i, s: (0, first + i)) for _, a in pieces]
    in_specs += [once(own.shape, (0, 0, 0))] + [once(g.shape, (0, 0)) for g in grads]
    args = [a for _, a in pieces] + [own, *grads, *after]
    in_specs += [ANYWHERE] * len(after)
    aliases = {}
    if before is not None:
        in_specs.append(ANYWHERE)
        args.append(before)
        aliases = {len(args): 0}
    return pl.pallas_call(
        functools.partial(weight_kernel, places, n_row, c),
        out_shape=jax.ShapeDtypeStruct(shape, BF16),
        grid_spec=pltpu.PrefetchScalarGridSpec(
            num_scalar_prefetch=1,
            grid=(count,),
            in_specs=in_specs,
            out_specs=pl.BlockSpec((tile, width), lambda i, s: (first + i, 0)),
            scratch_shapes=[pltpu.VMEM((rows, tile), BF16)],
        ),
        input_output_aliases=aliases,
        compiler_params=PARAMS,
        cost_estimate=cost(
            2 * rows * width * count * tile, rows * width + (rows + width) * count * tile
        ),
        name="weight_rows",
    )(where, *args)


def sums_kernel(counts, table_ref, *refs):
    at = 0
    for job, count in enumerate(counts):
        total = refs[at][...].astype(F32)
        for ref in refs[at + 1 : at + count]:
            total = total + ref[...].astype(F32)
        out_ref = refs[job - len(counts)]
        out_ref[...] = total.astype(BF16).reshape(out_ref.shape)
        at += count


def sums(table, going, ended, at, shape, before, after):
    parts = going + ended
    jobs = [part.job() for part in parts]
    steps = max(2, *(size for _, size in jobs)) if len(jobs) > 1 else max(2, jobs[0][1])
    in_specs, args, out_specs, out_shape, values = [], [], [], [], 0
    for part, (terms, size) in zip(parts, jobs):
        c, cuts = part.c, steps // size
        if c % (16 * cuts):
            cuts = 1
        block = (1, c // cuts, part.width)

        def index(i, table, first=0, by_slot=False, size=size, cuts=cuts):
            at = first + i * size // steps
            return (table[at] if by_slot else at, lax.rem(i, cuts), 0)

        for array, first, by_slot in terms:
            in_specs.append(
                pl.BlockSpec(block, functools.partial(index, first=first, by_slot=by_slot))
            )
            args.append(array)
        values += (len(terms) + 1) * size * c * part.width
        if part in going:
            out_specs.append(pl.BlockSpec(block, index))
            out_shape.append(jax.ShapeDtypeStruct((size, c, part.width), BF16))
        else:
            out_specs.append(
                pl.BlockSpec(
                    block[1:],
                    lambda i, table, h=block[1], cuts=cuts: (at // h + lax.rem(i, cuts), 0),
                )
            )
            out_shape.append(jax.ShapeDtypeStruct(shape, BF16))
    args += after
    in_specs += [ANYWHERE] * len(after)
    aliases = {}
    if ended and before is not None:
        args.append(before)
        in_specs.append(ANYWHERE)
        aliases = {len(args): len(going)}
    outs = pl.pallas_call(
        functools.partial(sums_kernel, [len(terms) for terms, _ in jobs]),
        out_shape=out_shape,
        grid_spec=pltpu.PrefetchScalarGridSpec(
            num_scalar_prefetch=1, grid=(steps,), in_specs=in_specs, out_specs=out_specs,
        ),
        input_output_aliases=aliases,
        compiler_params=PARAMS,
        cost_estimate=cost(values, values),
        name="sums",
    )(table, *args)
    for part, out in zip(going, outs):
        part.take(out)
    return outs[-1] if ended else before, [outs[0]]


class Halving:
    def __init__(self, send, keep, levels, n):
        self.levels, self.n = list(levels), n
        self.half, self.c, self.width = keep.shape
        received = flip(send, self.levels.pop(0), n)
        self.terms = [[keep, 0, True], [received, 0, True]]

    def take(self, out):
        self.terms.append([flip(out, self.levels.pop(0), self.n), 0, False])

    def job(self):
        size = self.half = self.half // 2 if self.levels else 1
        job = ([tuple(term) for term in self.terms], size)
        self.terms = [[array, first + size, by_slot] for array, first, by_slot in self.terms]
        return job


def hold_kernel(*refs):
    refs[-1][...] = jnp.zeros_like(refs[-1])


def hold(after):
    return pl.pallas_call(
        hold_kernel,
        out_shape=jax.ShapeDtypeStruct((8, 128), F32),
        grid=(1,),
        in_specs=[ANYWHERE] * len(after),
        out_specs=pl.BlockSpec((8, 128), lambda i: (0, 0)),
        compiler_params=PARAMS,
        cost_estimate=cost(50 * 10**9, 8 * 128),
        name="hold",
    )(*after)


def per_device(n_row, n_col, hidden_acts, out_grad, down_weight):
    tokens, units = hidden_acts.shape
    features = out_grad.shape[1]
    assert n_col == 2 * n_row and tokens % 32 == 0
    further = [1 << b for b in range(1, n_col.bit_length() - 1)]
    levels = [(1, 1), *zip(further, further[::-1])]
    kept = [halving_order([bits[h] for bits in levels[1:]]) for h in (0, 1)]
    c = tokens // 2
    tile = 128 * max(d for d in (1, 2, 4) if units % (128 * d) == 0)
    tiles = units // tile
    col, row = (lax.axis_index(axis).astype(jnp.int32) for axis in ("col", "row"))
    where = jnp.stack([col, row])
    order = jnp.where(col & 1, jnp.array(kept[1], jnp.int32), jnp.array(kept[0], jnp.int32))
    table = slot_of(row, col ^ order, n_row)

    own = out_grad.reshape(2, tokens, features)
    half = n_row // 2
    chunks = [own[:, :c], own[:, c:]]
    middle = [near_shift(chunks[0], half, n_row), None]
    others = {s: near_shift(own, s, n_row) for s in range(1, n_row) if s != half}

    whole = {bit: flip(hidden_acts, (bit, bit), n_col) for bit in further}

    turned, send0, keep0, send1, keep1 = turn_weights(where, own, down_weight, c, n_row, tile)
    middle[0], turned, chunks[1], arrived = lax.optimization_barrier(
        (middle[0], turned, chunks[1], list(whole.values()))
    )
    whole = dict(zip(whole, arrived))
    far0 = [far_shift(middle[0], e, n_row) for e in range(1, half)]
    middle[1] = near_shift(chunks[1], half, n_row)

    def near(k):
        return [middle[k] if s == half else others[s] for s in range(1, n_row)]

    corners = []
    for t, bits in enumerate(levels[1:]):
        passed = [((j0 ^ bits[0], j1 ^ bits[1]), flip(a, bits, n_col)) for (j0, j1), a in corners]
        corners = corners + passed
        if t < len(further) - 1:
            corners.append((bits, jnp.where(col & 1, whole[bits[1]], whole[bits[0]])))
    corners = [((j0, j1), a) for (j0, j1), a in corners if j0 not in whole]

    send0, keep0, grads0 = partial_sums(
        where, turned, near(0), far0, send0, keep0, 0, list(whole.values())
    )
    zero = Halving(send0, keep0, levels, n_col)

    middle[1], tied = lax.optimization_barrier((middle[1], send0))
    far1 = [far_shift(middle[1], e, n_row) for e in range(1, half)]
    pieces = [((0, 0), hidden_acts)] + [((j, j), a) for j, a in whole.items()] + corners
    pieces += [((j1 ^ 1, j0 ^ 1), flip(a, (1, 1), n_col)) for (j0, j1), a in pieces]
    exchanged = [a for _, a in pieces[n_col // 2 :]]

    hidden_grad, weight_grad, done = None, None, 0

    def advance(going, ended, at, after):
        nonlocal hidden_grad
        hidden_grad, after = sums(table, going, ended, at, (tokens, units), hidden_grad, after)
        return after

    def work(count, after):
        nonlocal weight_grad, done
        count = min(tiles - done, count)
        if count:
            weight_grad = weight_rows(
                where, pieces, own, [grads0, grads1], weight_grad, (units, features), n_row, c,
                tile, done, count, after,
            )
            done += count
        return [weight_grad]

    after = [hold([tied, middle[1]] + [a for _, a in corners])]
    after = advance([zero], [], 0, after)
    send1, keep1, grads1 = partial_sums(
        where, turned, near(1), far1, send1, keep1, 1, after + exchanged[:1]
    )
    one = Halving(send1, keep1, levels, n_col)
    after = work(3, [send1])
    parts, steps = [zero, one], len(levels) - 1
    for step in range(steps):
        going, ended = [p for p in parts if p.levels], [p for p in parts if not p.levels]
        after = advance(going, ended, 0, after)
        parts = going
        after = work(-(-(tiles - done) * 3 // (5 * (steps - step) - 4 if step < steps - 1 else 3)), after)
    advance([], [one], c, after)
    return weight_grad, hidden_grad


def solution(mesh):
    in_specs = (P("col", "row"), P("row", "col"), P("row", "col"))
    out_specs = (P("row", "col"), P("col", "row"))
    return jax.shard_map(
        functools.partial(per_device, mesh.shape["row"], mesh.shape["col"]),
        mesh=mesh, in_specs=in_specs, out_specs=out_specs, check_vma=False,
    )
```

```python
import functools

import jax
import jax.numpy as jnp
from jax import lax
from jax.experimental import pallas as pl
from jax.experimental.pallas import tpu as pltpu
from jax.sharding import PartitionSpec as P

F32, BF16 = jnp.float32, jnp.bfloat16
ANYWHERE = pl.BlockSpec(memory_space=pl.ANY)
CUTS = 4
PARAMS = pltpu.CompilerParams(vmem_limit_bytes=58 * 1024 * 1024)


def cost(flops, values):
    return pl.CostEstimate(flops=flops, bytes_accessed=2 * values, transcendentals=0)


def once(shape, index):
    return pl.BlockSpec(shape, lambda *_: index, pipeline_mode=pl.Buffered(1))


def halving_order(bits):
    if not bits:
        return [0]
    keep = halving_order(bits[1:])
    return [o ^ bits[0] for o in keep] + keep


def flip(x, bits, n):
    return lax.ppermute(x, "col", [(i, i ^ bits[i & 1]) for i in range(n)])


def shift(x, s, n):
    return lax.ppermute(x, "row", [(i, (i + s) % n) for i in range(n)])


def slot_of(row, owner, n_row):
    return lax.rem(row - owner // 2 - 1 + n_row, n_row)


def turn_kernel(c, where_ref, own_ref, *refs):
    w_refs, turned_ref, outs, mine = refs[:CUTS], refs[CUTS], refs[CUTS + 1 : -1], refs[-1]
    core = where_ref[0] & 1

    @pl.when(pl.program_id(0) == 0)
    def _():
        for p in range(4):
            h = core if p % 2 else 1 - core
            mine[pl.ds(p * c, c), :] = own_ref[h, pl.ds(p // 2 * c, c), :]

    res, width = None, mine.shape[1] // CUTS
    for q, w_ref in enumerate(w_refs):
        columns = pl.ds(q * width, width)
        turned = w_ref[...].T
        turned_ref[0, columns, :] = turned
        term = jnp.dot(mine[:, columns], turned, preferred_element_type=F32)
        res = term if res is None else res + term
    res = res.astype(BF16)
    for p, ref in enumerate(outs):
        ref[0] = res[p * c : (p + 1) * c]


def turn_weights(where, own, weight, c, n_row, tile):
    units, depth = weight.shape
    tiles = units // tile
    part = jax.ShapeDtypeStruct((n_row, c, units), BF16)
    part_spec = pl.BlockSpec((1, c, tile), lambda i, s: (n_row - 1, 0, i))
    return pl.pallas_call(
        functools.partial(turn_kernel, c),
        out_shape=(jax.ShapeDtypeStruct((tiles, depth, tile), BF16),) + (part,) * 4,
        grid_spec=pltpu.PrefetchScalarGridSpec(
            num_scalar_prefetch=1,
            grid=(tiles,),
            in_specs=[once(own.shape, (0, 0, 0))]
            + [pl.BlockSpec((tile, depth // CUTS), lambda i, s, q=q: (i, q)) for q in range(CUTS)],
            out_specs=(pl.BlockSpec((1, depth, tile), lambda i, s: (i, 0, 0)),) + (part_spec,) * 4,
            scratch_shapes=[pltpu.VMEM((4 * c, depth), BF16)],
        ),
        compiler_params=PARAMS,
        cost_estimate=cost(8 * c * depth * units, 2 * units * depth + 4 * c * units),
        name="turn_weights",
    )(where, own, *[weight] * CUTS)


def partial_kernel(n_row, c, where_ref, *refs):
    w_refs, others = refs[:CUTS], refs[CUTS : CUTS + n_row - 1]
    send_ref, keep_ref, rows_ref, lhs = refs[-4:]
    core, count = where_ref[0] & 1, (n_row - 1) * c

    @pl.when(pl.program_id(0) == 0)
    def _():
        for s, ref in enumerate(others):
            lhs[pl.ds(s * c, c), :] = ref[0, 1 - core]
            lhs[pl.ds(count + s * c, c), :] = ref[0, core]
        rows_ref[...] = lhs[...]

    res, width = None, lhs.shape[1] // CUTS
    for q, w_ref in enumerate(w_refs):
        term = jnp.dot(lhs[:, pl.ds(q * width, width)], w_ref[0], preferred_element_type=F32)
        res = term if res is None else res + term
    res = res.astype(BF16)
    send_ref[...] = res[:count].reshape(send_ref.shape)
    keep_ref[...] = res[count:].reshape(keep_ref.shape)


def partial_sums(where, turned, others, send, keep, after):
    n_row, c, units = send.shape
    tiles, depth, tile = turned.shape
    count = 2 * (n_row - 1) * c
    in_specs = [
        pl.BlockSpec((1, depth // CUTS, tile), lambda i, s, q=q: (i, q, 0)) for q in range(CUTS)
    ]
    if len(others) == 1:
        others = others * (n_row - 1)
        at = [lambda i, s, d=d: (lax.rem(s[1] - d + n_row, n_row), 0, 0, 0) for d in range(1, n_row)]
    else:
        others = [a[None] for a in others]
        at = [lambda i, s: (0, 0, 0, 0)] * len(others)
    in_specs += [pl.BlockSpec((1, 2, c, depth), index, pipeline_mode=pl.Buffered(1)) for index in at]
    in_specs += [ANYWHERE] * (2 + len(after))
    part = jax.ShapeDtypeStruct(send.shape, BF16)
    part_spec = pl.BlockSpec((n_row - 1, c, tile), lambda i, s: (0, 0, i))
    return pl.pallas_call(
        functools.partial(partial_kernel, n_row, c),
        out_shape=(part, part, jax.ShapeDtypeStruct((count, depth), BF16)),
        grid_spec=pltpu.PrefetchScalarGridSpec(
            num_scalar_prefetch=1,
            grid=(tiles,),
            in_specs=in_specs,
            out_specs=(part_spec, part_spec, pl.BlockSpec((count, depth), lambda i, s: (0, 0))),
            scratch_shapes=[pltpu.VMEM((count, depth), BF16)],
        ),
        input_output_aliases={1 + CUTS + len(others): 0, 2 + CUTS + len(others): 1},
        compiler_params=PARAMS,
        cost_estimate=cost(
            2 * count * depth * units, 2 * count * depth + units * depth + count * units
        ),
        name="partial_sums",
    )(where, *[turned] * CUTS, *others, send, keep, *after)


def weight_kernel(places, n_row, c, where_ref, *refs):
    acts_refs, refs = refs[: len(places)], refs[len(places):]
    own_ref, grads_refs = refs[0], refs[1:3]
    out_ref, acts, grads, sems = refs[-4:]
    me, row = where_ref[0], where_ref[1]
    core, tokens, count = me & 1, 2 * c, 2 * (n_row - 1) * c
    for (j0, j1), ref in zip(places, acts_refs):
        owner = me ^ jnp.where(core == 1, j1, j0)
        h = owner & 1
        slot = slot_of(row, owner, n_row) + jnp.where(h == core, n_row - 1, 0)
        for k in range(2):
            start = jnp.where(
                owner // 2 == row, 2 * count + h * tokens + k * c, k * count + slot * c
            )
            acts[pl.ds(pl.multiple_of(start, c), c), :] = ref[pl.ds(k * c, c), :]

    @pl.when(pl.program_id(0) == 0)
    def _():
        sources = [ref.at[pl.ds(i * tokens, tokens)] for ref in grads_refs for i in range(n_row - 1)]
        sources += [own_ref.at[h] for h in range(2)]
        copies = [
            pltpu.make_async_copy(source, grads.at[pl.ds(i * tokens, tokens)], sems.at[i])
            for i, source in enumerate(sources)
        ]
        for copy in copies:
            copy.start()
        for copy in copies:
            copy.wait()

    out_ref[...] = lax.dot_general(
        acts[...], grads[...], (((0,), (0,)), ((), ())), preferred_element_type=F32
    ).astype(BF16)


def weight_rows(where, pieces, own, grads, before, shape, n_row, c, tile, first, count, after):
    places = [place for place, _ in pieces]
    rows, width = 2 * n_row * 2 * c, shape[1]
    in_specs = [pl.BlockSpec((a.shape[0], tile), lambda i, s: (0, first + i)) for _, a in pieces]
    in_specs += [ANYWHERE] * 3
    args = [a for _, a in pieces] + [own, *grads, *after]
    in_specs += [ANYWHERE] * len(after)
    aliases = {}
    if before is not None:
        in_specs.append(ANYWHERE)
        args.append(before)
        aliases = {len(args): 0}
    return pl.pallas_call(
        functools.partial(weight_kernel, places, n_row, c),
        out_shape=jax.ShapeDtypeStruct(shape, BF16),
        grid_spec=pltpu.PrefetchScalarGridSpec(
            num_scalar_prefetch=1,
            grid=(count,),
            in_specs=in_specs,
            out_specs=pl.BlockSpec((tile, width), lambda i, s: (first + i, 0)),
            scratch_shapes=[
                pltpu.VMEM((rows, tile), BF16),
                pltpu.VMEM((rows, width), BF16),
                pltpu.SemaphoreType.DMA((2 * n_row,)),
            ],
        ),
        input_output_aliases=aliases,
        compiler_params=PARAMS,
        cost_estimate=cost(
            2 * rows * width * count * tile, rows * width + (rows + width) * count * tile
        ),
        name="weight_rows",
    )(where, *args)


def sums_kernel(counts, table_ref, *refs):
    at = 0
    for job, count in enumerate(counts):
        total = refs[at][...].astype(F32)
        for ref in refs[at + 1 : at + count]:
            total = total + ref[...].astype(F32)
        out_ref = refs[job - len(counts)]
        out_ref[...] = total.astype(BF16).reshape(out_ref.shape)
        at += count


def sums(table, going, ended, at, shape, before, after):
    parts = going + ended
    jobs = [part.job() for part in parts]
    steps = max(2, *(size for _, size in jobs)) if len(jobs) > 1 else max(2, jobs[0][1])
    in_specs, args, out_specs, out_shape, values = [], [], [], [], 0
    for part, (terms, size) in zip(parts, jobs):
        c, cuts = part.c, steps // size
        if c % (16 * cuts):
            cuts = 1
        block = (1, c // cuts, part.width)

        def index(i, table, first=0, by_slot=False, size=size, cuts=cuts):
            at = first + i * size // steps
            return (table[at] if by_slot else at, lax.rem(i, cuts), 0)

        for array, first, by_slot in terms:
            in_specs.append(
                pl.BlockSpec(block, functools.partial(index, first=first, by_slot=by_slot))
            )
            args.append(array)
        values += (len(terms) + 1) * size * c * part.width
        if part in going:
            out_specs.append(pl.BlockSpec(block, index))
            out_shape.append(jax.ShapeDtypeStruct((size, c, part.width), BF16))
        else:
            out_specs.append(
                pl.BlockSpec(
                    block[1:],
                    lambda i, table, h=block[1], cuts=cuts: (at // h + lax.rem(i, cuts), 0),
                )
            )
            out_shape.append(jax.ShapeDtypeStruct(shape, BF16))
    args += after
    in_specs += [ANYWHERE] * len(after)
    aliases = {}
    if ended and before is not None:
        args.append(before)
        in_specs.append(ANYWHERE)
        aliases = {len(args): len(going)}
    outs = pl.pallas_call(
        functools.partial(sums_kernel, [len(terms) for terms, _ in jobs]),
        out_shape=out_shape,
        grid_spec=pltpu.PrefetchScalarGridSpec(
            num_scalar_prefetch=1, grid=(steps,), in_specs=in_specs, out_specs=out_specs,
        ),
        input_output_aliases=aliases,
        compiler_params=PARAMS,
        cost_estimate=cost(values, values),
        name="sums",
    )(table, *args)
    for part, out in zip(going, outs):
        part.take(out)
    return outs[-1] if ended else before, [outs[0]]


class Halving:
    def __init__(self, send, keep, levels, n):
        self.levels, self.n = list(levels), n
        self.half, self.c, self.width = keep.shape
        received = flip(send, self.levels.pop(0), n)
        self.terms = [[keep, 0, True], [received, 0, True]]

    def take(self, out):
        self.terms.append([flip(out, self.levels.pop(0), self.n), 0, False])

    def job(self):
        size = self.half = self.half // 2 if self.levels else 1
        job = ([tuple(term) for term in self.terms], size)
        self.terms = [[array, first + size, by_slot] for array, first, by_slot in self.terms]
        return job


def hold_kernel(*refs):
    refs[-1][...] = jnp.zeros_like(refs[-1])


def hold(after):
    return pl.pallas_call(
        hold_kernel,
        out_shape=jax.ShapeDtypeStruct((8, 128), F32),
        grid=(1,),
        in_specs=[ANYWHERE] * len(after),
        out_specs=pl.BlockSpec((8, 128), lambda i: (0, 0)),
        compiler_params=PARAMS,
        cost_estimate=cost(50 * 10**9, 8 * 128),
        name="hold",
    )(*after)


def per_device(n_row, n_col, hidden_acts, out_grad, down_weight):
    tokens, units = hidden_acts.shape
    features = out_grad.shape[1]
    assert n_col == 2 * n_row and tokens % 32 == 0
    further = [1 << b for b in range(1, n_col.bit_length() - 1)]
    levels = [(1, 1), *zip(further, further[::-1])]
    kept = [halving_order([bits[h] for bits in levels[1:]]) for h in (0, 1)]
    c = tokens // 2
    tile = 128 * max(d for d in (1, 2, 4) if units % (128 * d) == 0)
    tiles = units // tile
    col, row = (lax.axis_index(axis).astype(jnp.int32) for axis in ("col", "row"))
    where = jnp.stack([col, row])
    order = jnp.where(col & 1, jnp.array(kept[1], jnp.int32), jnp.array(kept[0], jnp.int32))
    table = slot_of(row, col ^ order, n_row)

    own = out_grad.reshape(2, tokens, features)
    chunks = [own[:, :c], own[:, c:]]
    others0 = [shift(chunks[0], s, n_row) for s in range(1, n_row)]

    whole = {bit: flip(hidden_acts, (bit, bit), n_col) for bit in further}

    turned, send0, keep0, send1, keep1 = turn_weights(where, own, down_weight, c, n_row, tile)
    turned, chunks[1] = lax.optimization_barrier((turned, chunks[1]))
    turned, arrived, others0 = lax.optimization_barrier((turned, list(whole.values()), others0))
    whole = dict(zip(whole, arrived))

    corners = []
    for t, bits in enumerate(levels[1:]):
        passed = [((j0 ^ bits[0], j1 ^ bits[1]), flip(a, bits, n_col)) for (j0, j1), a in corners]
        corners = corners + passed
        if t < len(further) - 1:
            corners.append((bits, jnp.where(col & 1, whole[bits[1]], whole[bits[0]])))
    corners = [((j0, j1), a) for (j0, j1), a in corners if j0 not in whole]

    others1 = [lax.all_gather(chunks[1], "row")]
    send0, keep0, grads0 = partial_sums(where, turned, others0, send0, keep0, [])
    zero = Halving(send0, keep0, levels, n_col)

    pieces = [((0, 0), hidden_acts)] + [((j, j), a) for j, a in whole.items()] + corners
    pieces += [((j1 ^ 1, j0 ^ 1), flip(a, (1, 1), n_col)) for (j0, j1), a in pieces]
    exchanged = [a for _, a in pieces[n_col // 2 :]]

    hidden_grad, weight_grad, done = None, None, 0

    def advance(going, ended, at, after):
        nonlocal hidden_grad
        hidden_grad, after = sums(table, going, ended, at, (tokens, units), hidden_grad, after)
        return after

    def work(count, after):
        nonlocal weight_grad, done
        count = min(tiles - done, count)
        if count:
            weight_grad = weight_rows(
                where, pieces, own, [grads0, grads1], weight_grad, (units, features), n_row, c,
                tile, done, count, after,
            )
            done += count
        return [weight_grad]

    after = [hold([send0] + [a for _, a in corners])]
    after = advance([zero], [], 0, after)
    send1, keep1, grads1 = partial_sums(
        where, turned, others1, send1, keep1, after + exchanged
    )
    one = Halving(send1, keep1, levels, n_col)
    after = work(3, [send1, zero.terms[-1][0]])
    parts, steps = [zero, one], len(levels) - 1
    for step in range(steps):
        going, ended = [p for p in parts if p.levels], [p for p in parts if not p.levels]
        after = advance(going, ended, 0, after)
        parts = going
        after = work(-(-(tiles - done) * 3 // (5 * (steps - step) - 4 if step < steps - 1 else 3)), after)
    advance([], [one], c, after)
    return weight_grad, hidden_grad


def solution(mesh):
    in_specs = (P("col", "row"), P("row", "col"), P("row", "col"))
    out_specs = (P("row", "col"), P("col", "row"))
    return jax.shard_map(
        functools.partial(per_device, mesh.shape["row"], mesh.shape["col"]),
        mesh=mesh, in_specs=in_specs, out_specs=out_specs, check_vma=False,
    )
```

```python
import functools

import jax
import jax.numpy as jnp
from jax import lax
from jax.experimental import pallas as pl
from jax.experimental.pallas import tpu as pltpu
from jax.sharding import PartitionSpec as P

F32, BF16 = jnp.float32, jnp.bfloat16
ANYWHERE = pl.BlockSpec(memory_space=pl.ANY)
PARAMS = pltpu.CompilerParams(vmem_limit_bytes=40 * 1024 * 1024)


def cost(flops, values):
    return pl.CostEstimate(flops=flops, bytes_accessed=2 * values, transcendentals=0)


def halving_order(bits):
    if not bits:
        return [0]
    keep = halving_order(bits[1:])
    return [o ^ bits[0] for o in keep] + keep


def flip(x, bits, n):
    return lax.ppermute(x, "col", [(i, i ^ bits[i & 1]) for i in range(n)])


def doubled(x, bits, n):
    held = {0: x}
    for bit in bits:
        pairs = [(i, i ^ bit) for i in range(n)]
        for j in list(held):
            held[j ^ bit] = lax.ppermute(held[j], "row", pairs)
    return held


def assemble_kernel(rows_of, orders, c, where_ref, *refs):
    grads_ref, turned_ref, rel = refs[-3:]
    me, row = where_ref[0], where_ref[1]
    for j, ref in zip(rows_of, refs):
        rows = ref.shape[0]
        grads_ref[pl.ds(pl.multiple_of((row ^ j) * rows, rows), rows), :] = ref[...]
    for p, (j0, j1) in enumerate(zip(*orders)):
        start = pl.multiple_of((me ^ jnp.where(me & 1, j1, j0)) * c, c)
        rel[pl.ds(p * c, c), :] = grads_ref[pl.ds(start, c), :]
    turned_ref[...] = rel[...].T


def assemble(where, blocks, orders, c, after):
    rows_of, arrays = list(blocks), list(blocks.values())
    depth, rows = arrays[0].shape[1], len(orders[0]) * c
    steps = 2
    part = pl.BlockSpec((arrays[0].shape[0], depth // steps), lambda i, s: (0, i))
    return pl.pallas_call(
        functools.partial(assemble_kernel, rows_of, orders, c),
        out_shape=(
            jax.ShapeDtypeStruct((rows, depth), BF16),
            jax.ShapeDtypeStruct((depth, rows), BF16),
        ),
        grid_spec=pltpu.PrefetchScalarGridSpec(
            num_scalar_prefetch=1,
            grid=(steps,),
            in_specs=[part] * len(arrays) + [ANYWHERE] * len(after),
            out_specs=(
                pl.BlockSpec((rows, depth // steps), lambda i, s: (0, i)),
                pl.BlockSpec((depth // steps, rows), lambda i, s: (i, 0)),
            ),
            scratch_shapes=[pltpu.VMEM((rows, depth // steps), BF16)],
        ),
        compiler_params=PARAMS,
        cost_estimate=cost(0, 3 * rows * depth),
        name="assemble",
    )(where, *arrays, *after)


def partial_kernel(w_ref, g_ref, *refs):
    send_ref, keep_ref = refs[-2:]
    res = jnp.dot(w_ref[...], g_ref[...], preferred_element_type=F32).astype(BF16).T
    rows = res.shape[0] // 2
    send_ref[...] = res[:rows].reshape(send_ref.shape)
    keep_ref[...] = res[rows:].reshape(keep_ref.shape)


def partial_sums(turned, weight, n, c, tile, first, count, after):
    depth = weight.shape[1]
    out = jax.ShapeDtypeStruct((n // 2, c, count * tile), BF16)
    out_spec = pl.BlockSpec((n // 2, c, tile), lambda i: (0, 0, i))
    return pl.pallas_call(
        partial_kernel,
        out_shape=(out, out),
        grid=(count,),
        in_specs=[
            pl.BlockSpec((tile, depth), lambda i: (first + i, 0)),
            pl.BlockSpec((depth, n * c), lambda i: (0, 0), pipeline_mode=pl.Buffered(1)),
        ]
        + [ANYWHERE] * len(after),
        out_specs=(out_spec, out_spec),
        compiler_params=PARAMS,
        cost_estimate=cost(
            2 * n * c * depth * count * tile,
            n * c * depth + count * tile * depth + n * c * count * tile,
        ),
        name="partial_sums",
    )(weight, turned, *after)


def weight_kernel(places, chunks, n, where_ref, *refs):
    acts_refs, refs = refs[: len(places)], refs[len(places):]
    grads_refs, out_ref, acts = refs[: len(chunks)], refs[-2], refs[-1]
    me = where_ref[0]
    for (j0, j1), ref in zip(places, acts_refs):
        owner = me ^ jnp.where(me & 1, j1, j0)
        for at, c in chunks:
            start = pl.multiple_of(at * n + owner * c, c)
            acts[pl.ds(start, c), :] = ref[pl.ds(at, c), :]
    total = None
    for (at, c), ref in zip(chunks, grads_refs):
        term = lax.dot_general(
            acts[pl.ds(at * n, c * n), :], ref[...],
            (((0,), (0,)), ((), ())), preferred_element_type=F32,
        )
        total = term if total is None else total + term
    out_ref[...] = total.astype(BF16)


def weight_rows(where, pieces, grads, chunks, n, before, shape, tile, first, count, after):
    places = [place for place, _ in pieces]
    rows, width = sum(g.shape[0] for g in grads), shape[1]
    in_specs = [pl.BlockSpec((a.shape[0], tile), lambda i, s: (0, first + i)) for _, a in pieces]
    in_specs += [
        pl.BlockSpec(g.shape, lambda i, s: (0, 0), pipeline_mode=pl.Buffered(1)) for g in grads
    ]
    args = [a for _, a in pieces] + list(grads) + list(after)
    in_specs += [ANYWHERE] * len(after)
    aliases = {}
    if before is not None:
        in_specs.append(ANYWHERE)
        args.append(before)
        aliases = {len(args): 0}
    return pl.pallas_call(
        functools.partial(weight_kernel, places, chunks, n),
        out_shape=jax.ShapeDtypeStruct(shape, BF16),
        grid_spec=pltpu.PrefetchScalarGridSpec(
            num_scalar_prefetch=1,
            grid=(count,),
            in_specs=in_specs,
            out_specs=pl.BlockSpec((tile, width), lambda i, s: (first + i, 0)),
            scratch_shapes=[pltpu.VMEM((rows, tile), BF16)],
        ),
        input_output_aliases=aliases,
        compiler_params=PARAMS,
        cost_estimate=cost(
            2 * rows * width * count * tile, rows * width + (rows + width) * count * tile
        ),
        name="weight_rows",
    )(where, *args)


def sums_kernel(jobs, n_final, *refs):
    n_out = len(jobs) - n_final + (n_final > 0)
    outs, base = refs[-n_out:], 0
    at = 0
    for job, (width, cuts, spans) in enumerate(jobs):
        for lo, hi in zip(cuts, cuts[1:]):
            total = None
            for (begin, end), ref in zip(spans, refs[at : at + len(spans)]):
                if begin <= lo and hi <= end:
                    term = ref[:, :, lo - begin : hi - begin].astype(F32)
                    total = term if total is None else total + term
            if job < n_out - (n_final > 0):
                outs[job][:, :, lo:hi] = total.astype(BF16)
            else:
                outs[-1][:, base + lo : base + hi] = total[0].astype(BF16)
        if job >= len(jobs) - n_final:
            base += width
        at += len(spans)


def sums(going, ended, at, shape, before, after):
    parts = going + ended
    jobs = [part.job() for part in parts]
    steps = min(2, min(part.c for part in parts) // 16)
    in_specs, args, out_specs, out_shape, values = [], [], [], [], 0
    for part, (terms, size) in zip(parts, jobs):
        for array, first, _ in terms:
            in_specs.append(
                pl.BlockSpec(
                    (size, part.c // steps, array.shape[2]),
                    lambda i, b=first // size: (b, i, 0),
                )
            )
            args.append(array)
        values += (len(terms) + 1) * size * part.c * part.width
        if part in going:
            out_specs.append(pl.BlockSpec((size, part.c // steps, part.width), lambda i: (0, i, 0)))
            out_shape.append(jax.ShapeDtypeStruct((size, part.c, part.width), BF16))
    args += after
    in_specs += [ANYWHERE] * len(after)
    aliases = {}
    if ended:
        height = ended[0].c // steps
        out_specs.append(pl.BlockSpec((height, shape[1]), lambda i: (at // height + i, 0)))
        out_shape.append(jax.ShapeDtypeStruct(shape, BF16))
        if before is not None:
            aliases = {len(args): len(going)}
            args.append(before)
            in_specs.append(ANYWHERE)
    layout = [
        (part.width, part.cuts, [span for _, _, span in terms])
        for part, (terms, _) in zip(parts, jobs)
    ]
    outs = pl.pallas_call(
        functools.partial(sums_kernel, layout, len(ended)),
        out_shape=out_shape,
        grid=(steps,),
        in_specs=in_specs,
        out_specs=out_specs,
        input_output_aliases=aliases,
        compiler_params=PARAMS,
        cost_estimate=cost(values, values),
        name="sums",
    )(*args)
    for part, out in zip(going, outs):
        part.take(out)
    return outs[-1] if ended else before, [outs[0]]


class Halving:
    def __init__(self, sends, keeps, levels, n):
        self.levels, self.n = list(levels), n
        self.half, self.c = keeps[0].shape[:2]
        self.cuts = [0]
        for keep in keeps:
            self.cuts.append(self.cuts[-1] + keep.shape[2])
        self.width = self.cuts[-1]
        spans = list(zip(self.cuts, self.cuts[1:]))
        bits = self.levels.pop(0)
        self.terms = [[keep, 0, span] for keep, span in zip(keeps, spans)]
        self.terms += [[flip(send, bits, n), 0, span] for send, span in zip(sends, spans)]

    def take(self, out):
        self.terms.append([flip(out, self.levels.pop(0), self.n), 0, (0, self.width)])

    def job(self):
        size = self.half = self.half // 2 if self.levels else 1
        job = ([tuple(term) for term in self.terms], size)
        self.terms = [[array, first + size, span] for array, first, span in self.terms]
        return job


def hold_kernel(*refs):
    refs[-1][...] = jnp.zeros_like(refs[-1])


def hold(after):
    return pl.pallas_call(
        hold_kernel,
        out_shape=jax.ShapeDtypeStruct((8, 128), F32),
        grid=(1,),
        in_specs=[ANYWHERE] * len(after),
        out_specs=pl.BlockSpec((8, 128), lambda i: (0, 0)),
        compiler_params=PARAMS,
        cost_estimate=cost(50 * 10**9, 8 * 128),
        name="hold",
    )(*after)


def per_device(n_row, n_col, hidden_acts, out_grad, down_weight):
    tokens, units = hidden_acts.shape
    features = out_grad.shape[1]
    owners = n_col // n_row
    further = [1 << b for b in range(1, n_col.bit_length() - 1)]
    levels = [(1, 1), *zip(further, further[::-1])]
    kept = [halving_order([bits[h] for bits in levels[1:]]) for h in (0, 1)]
    orders = [[o ^ 1 for o in kept[1 - h]] + kept[h] for h in (0, 1)]
    c = tokens // 2
    chunks = [(0, c), (c, c)]
    tile = 128 * max(d for d in (1, 2, 4) if units % (128 * d) == 0)
    tiles = units // tile
    cut = (tiles + 1) // 2
    col, row = lax.axis_index("col"), lax.axis_index("row")
    where = jnp.stack([col, row]).astype(jnp.int32)

    whole = {bit: flip(hidden_acts, (bit, bit), n_col) for bit in further}

    by_owner = out_grad.reshape(owners, tokens, features)

    def chunk(grads, k):
        at, c = chunks[k]
        return grads[:, at : at + c].reshape(owners * c, features)

    own = [chunk(by_owner, 0)]

    row_bits = [1 << b for b in reversed(range(n_row.bit_length() - 1))]
    last = [(i, i ^ row_bits[-1]) for i in range(n_row)]

    def most(x):
        held = doubled(x, row_bits[:-1], n_row)
        return {**held, row_bits[-1]: lax.ppermute(x, "row", last)}

    def rest(held):
        more = {j ^ row_bits[-1]: a for j, a in held.items() if j not in (0, row_bits[-1])}
        return {**held, **{j: lax.ppermute(a, "row", last) for j, a in more.items()}}

    first = most(own[0])
    far, later = lax.optimization_barrier((first[row_bits[0]], by_owner))
    own.append(chunk(later, 1))
    first[row_bits[0]] = far
    first = rest(first)
    second = most(own[1])

    grads0, turned0 = assemble(where, first, orders, c, list(whole.values()))

    corners = []
    for t, bits in enumerate(levels[1:]):
        passed = [((j0 ^ bits[0], j1 ^ bits[1]), flip(a, bits, n_col)) for (j0, j1), a in corners]
        if t < len(further) - 1:
            mine = jnp.where(col & 1, whole[bits[1]], whole[bits[0]])
            corners = corners + passed + [(bits, mine)]
        else:
            corners = corners + passed
    corners = [((j0, j1), a) for (j0, j1), a in corners if j0 not in whole]

    def partials(turned, first, count, after):
        send, keep = partial_sums(turned, down_weight, n_col, c, tile, first, count, after)
        return send, keep, [send]

    send, keep, after = partials(turned0, 0, tiles, [])
    zero = Halving([send], [keep], levels, n_col)

    second, tied = lax.optimization_barrier((second, after[0]))
    arrived = [a for j, a in second.items() if j]
    second = rest(second)
    pieces = [((0, 0), hidden_acts)] + [((j, j), a) for j, a in whole.items()] + corners
    pieces += [((j1 ^ 1, j0 ^ 1), flip(a, (1, 1), n_col)) for (j0, j1), a in pieces]

    hidden_grad, weight_grad, done = None, None, 0

    def advance(going, ended, at, after):
        nonlocal hidden_grad
        hidden_grad, after = sums(going, ended, at, (tokens, units), hidden_grad, after)
        return after

    def work(count, after):
        nonlocal weight_grad, done
        count = min(tiles - done, count)
        if count:
            weight_grad = weight_rows(
                where, pieces, grads, chunks, n_col, weight_grad, (units, features), tile,
                done, count, after,
            )
            done += count
        return [weight_grad]

    after = [hold([tied] + arrived + [a for _, a in corners])]
    after = advance([zero], [], 0, after)
    exchanged = [a for _, a in pieces[n_col // 2 :]]
    grads1, turned1 = assemble(where, second, orders, c, after + exchanged[:1])
    grads = [grads0, grads1]
    send_a, keep_a, after = partials(turned1, 0, cut, after)
    a1 = Halving([send_a], [keep_a], levels, n_col)
    send_b, keep_b, after = partials(turned1, cut, tiles - cut, after)
    b1 = Halving([send_b], [keep_b], levels, n_col)
    after = advance([zero, a1], [], 0, after)
    after = work(2, after)
    after = advance([b1], [], 0, after)
    parts, steps = [zero, a1, b1], len(levels) - 1
    for step in range(steps):
        after = work(-(-(tiles - done) // (steps - step)), after)
        going, ended = [p for p in parts if p.levels], [p for p in parts if not p.levels]
        after = advance(going, ended, 0 if zero in ended else c, after)
        parts = going
    return weight_grad, hidden_grad


def solution(mesh):
    in_specs = (P("col", "row"), P("row", "col"), P("row", "col"))
    out_specs = (P("row", "col"), P("col", "row"))
    return jax.shard_map(
        functools.partial(per_device, mesh.shape["row"], mesh.shape["col"]),
        mesh=mesh, in_specs=in_specs, out_specs=out_specs, check_vma=False,
    )
```

```python
import functools

import jax
import jax.numpy as jnp
from jax import lax
from jax.experimental import pallas as pl
from jax.experimental.pallas import tpu as pltpu
from jax.sharding import PartitionSpec as P

F32, BF16 = jnp.float32, jnp.bfloat16
ANYWHERE = pl.BlockSpec(memory_space=pl.ANY)
PARAMS = pltpu.CompilerParams(vmem_limit_bytes=60 * 1024 * 1024)


def cost(flops, values):
    return pl.CostEstimate(flops=flops, bytes_accessed=2 * values, transcendentals=0)


def halving_order(bits):
    if not bits:
        return [0]
    keep = halving_order(bits[1:])
    return [o ^ bits[0] for o in keep] + keep


def flip(x, bits, n):
    return lax.ppermute(x, "col", [(i, i ^ bits[i & 1]) for i in range(n)])


def doubled(x, bits, n):
    held = {0: x}
    for bit in bits:
        pairs = [(i, i ^ bit) for i in range(n)]
        for j in list(held):
            held[j ^ bit] = lax.ppermute(held[j], "row", pairs)
    return held


def assemble_kernel(rows_of, orders, c, where_ref, *refs):
    grads_ref, turned_ref, rel = refs[-3:]
    me, row = where_ref[0], where_ref[1]
    for j, ref in zip(rows_of, refs):
        rows = ref.shape[0]
        grads_ref[pl.ds(pl.multiple_of((row ^ j) * rows, rows), rows), :] = ref[...]
    for p, (j0, j1) in enumerate(zip(*orders)):
        start = pl.multiple_of((me ^ jnp.where(me & 1, j1, j0)) * c, c)
        rel[pl.ds(p * c, c), :] = grads_ref[pl.ds(start, c), :]
    turned_ref[...] = rel[...].T


def assemble(where, blocks, orders, c, after):
    rows_of, arrays = list(blocks), list(blocks.values())
    depth, rows = arrays[0].shape[1], len(orders[0]) * c
    steps = 2
    part = pl.BlockSpec((arrays[0].shape[0], depth // steps), lambda i, s: (0, i))
    return pl.pallas_call(
        functools.partial(assemble_kernel, rows_of, orders, c),
        out_shape=(
            jax.ShapeDtypeStruct((rows, depth), BF16),
            jax.ShapeDtypeStruct((depth, rows), BF16),
        ),
        grid_spec=pltpu.PrefetchScalarGridSpec(
            num_scalar_prefetch=1,
            grid=(steps,),
            in_specs=[part] * len(arrays) + [ANYWHERE] * len(after),
            out_specs=(
                pl.BlockSpec((rows, depth // steps), lambda i, s: (0, i)),
                pl.BlockSpec((depth // steps, rows), lambda i, s: (i, 0)),
            ),
            scratch_shapes=[pltpu.VMEM((rows, depth // steps), BF16)],
        ),
        compiler_params=PARAMS,
        cost_estimate=cost(0, 3 * rows * depth),
        name="assemble",
    )(where, *arrays, *after)


def partial_kernel(w_ref, g_ref, *refs):
    send_ref, keep_ref = refs[-2:]
    res = jnp.dot(w_ref[...], g_ref[...], preferred_element_type=F32).astype(BF16).T
    rows = res.shape[0] // 2
    send_ref[...] = res[:rows].reshape(send_ref.shape)
    keep_ref[...] = res[rows:].reshape(keep_ref.shape)


def partial_sums(turned, weight, n, c, tile, first, count, after):
    depth = weight.shape[1]
    out = jax.ShapeDtypeStruct((n // 2, c, count * tile), BF16)
    out_spec = pl.BlockSpec((n // 2, c, tile), lambda i: (0, 0, i))
    return pl.pallas_call(
        partial_kernel,
        out_shape=(out, out),
        grid=(count,),
        in_specs=[
            pl.BlockSpec((tile, depth), lambda i: (first + i, 0)),
            pl.BlockSpec((depth, n * c), lambda i: (0, 0), pipeline_mode=pl.Buffered(1)),
        ]
        + [ANYWHERE] * len(after),
        out_specs=(out_spec, out_spec),
        compiler_params=PARAMS,
        cost_estimate=cost(
            2 * n * c * depth * count * tile,
            n * c * depth + count * tile * depth + n * c * count * tile,
        ),
        name="partial_sums",
    )(weight, turned, *after)


def weight_kernel(places, chunks, n, where_ref, *refs):
    acts_refs, refs = refs[: len(places)], refs[len(places):]
    grads_refs, out_ref, acts = refs[: len(chunks)], refs[-2], refs[-1]
    me = where_ref[0]
    for (j0, j1), ref in zip(places, acts_refs):
        owner = me ^ jnp.where(me & 1, j1, j0)
        for at, c in chunks:
            start = pl.multiple_of(at * n + owner * c, c)
            acts[pl.ds(start, c), :] = ref[pl.ds(at, c), :]
    total = None
    for (at, c), ref in zip(chunks, grads_refs):
        term = lax.dot_general(
            acts[pl.ds(at * n, c * n), :], ref[...],
            (((0,), (0,)), ((), ())), preferred_element_type=F32,
        )
        total = term if total is None else total + term
    out_ref[...] = total.astype(BF16)


def weight_rows(where, pieces, grads, chunks, n, before, shape, tile, first, count, after):
    places = [place for place, _ in pieces]
    rows, width = sum(g.shape[0] for g in grads), shape[1]
    in_specs = [pl.BlockSpec((a.shape[0], tile), lambda i, s: (0, first + i)) for _, a in pieces]
    in_specs += [
        pl.BlockSpec(g.shape, lambda i, s: (0, 0), pipeline_mode=pl.Buffered(1)) for g in grads
    ]
    args = [a for _, a in pieces] + list(grads) + list(after)
    in_specs += [ANYWHERE] * len(after)
    aliases = {}
    if before is not None:
        in_specs.append(ANYWHERE)
        args.append(before)
        aliases = {len(args): 0}
    return pl.pallas_call(
        functools.partial(weight_kernel, places, chunks, n),
        out_shape=jax.ShapeDtypeStruct(shape, BF16),
        grid_spec=pltpu.PrefetchScalarGridSpec(
            num_scalar_prefetch=1,
            grid=(count,),
            in_specs=in_specs,
            out_specs=pl.BlockSpec((tile, width), lambda i, s: (first + i, 0)),
            scratch_shapes=[pltpu.VMEM((rows, tile), BF16)],
        ),
        input_output_aliases=aliases,
        compiler_params=PARAMS,
        cost_estimate=cost(
            2 * rows * width * count * tile, rows * width + (rows + width) * count * tile
        ),
        name="weight_rows",
    )(where, *args)


def sums_kernel(jobs, n_final, *refs):
    n_out = len(jobs) - n_final + (n_final > 0)
    outs, base = refs[-n_out:], 0
    at = 0
    for job, (width, cuts, spans) in enumerate(jobs):
        for lo, hi in zip(cuts, cuts[1:]):
            total = None
            for (begin, end), ref in zip(spans, refs[at : at + len(spans)]):
                if begin <= lo and hi <= end:
                    term = ref[:, :, lo - begin : hi - begin].astype(F32)
                    total = term if total is None else total + term
            if job < n_out - (n_final > 0):
                outs[job][:, :, lo:hi] = total.astype(BF16)
            else:
                outs[-1][:, base + lo : base + hi] = total[0].astype(BF16)
        if job >= len(jobs) - n_final:
            base += width
        at += len(spans)


def sums(going, ended, at, shape, before, after):
    parts = going + ended
    jobs = [part.job() for part in parts]
    steps = min(2, min(part.c for part in parts) // 16)
    in_specs, args, out_specs, out_shape, values = [], [], [], [], 0
    for part, (terms, size) in zip(parts, jobs):
        for array, first, _ in terms:
            in_specs.append(
                pl.BlockSpec(
                    (size, part.c // steps, array.shape[2]),
                    lambda i, b=first // size: (b, i, 0),
                )
            )
            args.append(array)
        values += (len(terms) + 1) * size * part.c * part.width
        if part in going:
            out_specs.append(pl.BlockSpec((size, part.c // steps, part.width), lambda i: (0, i, 0)))
            out_shape.append(jax.ShapeDtypeStruct((size, part.c, part.width), BF16))
    args += after
    in_specs += [ANYWHERE] * len(after)
    aliases = {}
    if ended:
        height = ended[0].c // steps
        out_specs.append(pl.BlockSpec((height, shape[1]), lambda i: (at // height + i, 0)))
        out_shape.append(jax.ShapeDtypeStruct(shape, BF16))
        if before is not None:
            aliases = {len(args): len(going)}
            args.append(before)
            in_specs.append(ANYWHERE)
    layout = [
        (part.width, part.cuts, [span for _, _, span in terms])
        for part, (terms, _) in zip(parts, jobs)
    ]
    outs = pl.pallas_call(
        functools.partial(sums_kernel, layout, len(ended)),
        out_shape=out_shape,
        grid=(steps,),
        in_specs=in_specs,
        out_specs=out_specs,
        input_output_aliases=aliases,
        compiler_params=PARAMS,
        cost_estimate=cost(values, values),
        name="sums",
    )(*args)
    for part, out in zip(going, outs):
        part.take(out)
    return outs[-1] if ended else before, [outs[0]]


class Halving:
    def __init__(self, sends, keeps, levels, n):
        self.levels, self.n = list(levels), n
        self.half, self.c = keeps[0].shape[:2]
        self.cuts = [0]
        for keep in keeps:
            self.cuts.append(self.cuts[-1] + keep.shape[2])
        self.width = self.cuts[-1]
        spans = list(zip(self.cuts, self.cuts[1:]))
        bits = self.levels.pop(0)
        self.terms = [[keep, 0, span] for keep, span in zip(keeps, spans)]
        self.terms += [[flip(send, bits, n), 0, span] for send, span in zip(sends, spans)]

    def take(self, out):
        self.terms.append([flip(out, self.levels.pop(0), self.n), 0, (0, self.width)])

    def job(self):
        size = self.half = self.half // 2 if self.levels else 1
        job = ([tuple(term) for term in self.terms], size)
        self.terms = [[array, first + size, span] for array, first, span in self.terms]
        return job


def hold_kernel(*refs):
    refs[-1][...] = jnp.zeros_like(refs[-1])


def hold(after):
    return pl.pallas_call(
        hold_kernel,
        out_shape=jax.ShapeDtypeStruct((8, 128), F32),
        grid=(1,),
        in_specs=[ANYWHERE] * len(after),
        out_specs=pl.BlockSpec((8, 128), lambda i: (0, 0)),
        compiler_params=PARAMS,
        cost_estimate=cost(50 * 10**9, 8 * 128),
        name="hold",
    )(*after)


def per_device(n_row, n_col, hidden_acts, out_grad, down_weight):
    tokens, units = hidden_acts.shape
    features = out_grad.shape[1]
    owners = n_col // n_row
    further = [1 << b for b in range(1, n_col.bit_length() - 1)]
    levels = [(1, 1), *zip(further, further[::-1])]
    kept = [halving_order([bits[h] for bits in levels[1:]]) for h in (0, 1)]
    orders = [[o ^ 1 for o in kept[1 - h]] + kept[h] for h in (0, 1)]
    c = tokens // 2
    chunks = [(0, c), (c, c)]
    lanes = units // 128
    tile, wide = (128 * max(d for d in range(1, most + 1) if lanes % d == 0) for most in (4, 13))
    tiles = units // tile
    col, row = lax.axis_index("col"), lax.axis_index("row")
    where = jnp.stack([col, row]).astype(jnp.int32)

    whole = {bit: flip(hidden_acts, (bit, bit), n_col) for bit in further}

    by_owner = out_grad.reshape(owners, tokens, features)

    def chunk(grads, k):
        at, c = chunks[k]
        return grads[:, at : at + c].reshape(owners * c, features)

    own = [chunk(by_owner, 0)]

    row_bits = [1 << b for b in reversed(range(n_row.bit_length() - 1))]
    last = [(i, i ^ row_bits[-1]) for i in range(n_row)]

    def most(x):
        held = doubled(x, row_bits[:-1], n_row)
        return {**held, row_bits[-1]: lax.ppermute(x, "row", last)}

    def rest(held):
        more = {j ^ row_bits[-1]: a for j, a in held.items() if j not in (0, row_bits[-1])}
        return {**held, **{j: lax.ppermute(a, "row", last) for j, a in more.items()}}

    first = most(own[0])
    far, later = lax.optimization_barrier((first[row_bits[0]], by_owner))
    own.append(chunk(later, 1))
    first[row_bits[0]] = far
    first = rest(first)
    second = most(own[1])

    grads0, turned0 = assemble(where, first, orders, c, list(whole.values()))

    corners = []
    for t, bits in enumerate(levels[1:]):
        passed = [((j0 ^ bits[0], j1 ^ bits[1]), flip(a, bits, n_col)) for (j0, j1), a in corners]
        if t < len(further) - 1:
            mine = jnp.where(col & 1, whole[bits[1]], whole[bits[0]])
            corners = corners + passed + [(bits, mine)]
        else:
            corners = corners + passed
    corners = [((j0, j1), a) for (j0, j1), a in corners if j0 not in whole]

    def partials(turned, first, count, after):
        send, keep = partial_sums(turned, down_weight, n_col, c, wide, first, count, after)
        return send, keep, [send]

    count = units // wide
    cut = (count + 1) // 2
    send, keep, after = partials(turned0, 0, count, [])
    zero = Halving([send], [keep], levels, n_col)

    second, tied = lax.optimization_barrier((second, after[0]))
    arrived = [a for j, a in second.items() if j]
    second = rest(second)
    pieces = [((0, 0), hidden_acts)] + [((j, j), a) for j, a in whole.items()] + corners
    pieces += [((j1 ^ 1, j0 ^ 1), flip(a, (1, 1), n_col)) for (j0, j1), a in pieces]

    hidden_grad, weight_grad, done = None, None, 0

    def advance(going, ended, at, after):
        nonlocal hidden_grad
        hidden_grad, after = sums(going, ended, at, (tokens, units), hidden_grad, after)
        return after

    def work(count, after):
        nonlocal weight_grad, done
        count = min(tiles - done, count)
        if count:
            weight_grad = weight_rows(
                where, pieces, grads, chunks, n_col, weight_grad, (units, features), tile,
                done, count, after,
            )
            done += count
        return [weight_grad]

    after = [hold([tied] + arrived + [a for _, a in corners])]
    after = advance([zero], [], 0, after)
    exchanged = [a for _, a in pieces[n_col // 2 :]]
    grads1, turned1 = assemble(where, second, orders, c, after + exchanged[:1])
    grads = [grads0, grads1]
    sends, keeps = [], []
    for first, last in ((0, cut), (cut, count)):
        if first < last:
            send, keep, after = partials(turned1, first, last - first, after)
            sends.append(send)
            keeps.append(keep)
    one = Halving(sends, keeps, levels, n_col)
    after = work(3, after)
    parts, steps = [zero, one], len(levels) - 1
    for step in range(steps):
        going, ended = [p for p in parts if p.levels], [p for p in parts if not p.levels]
        after = advance(going, ended, 0, after)
        parts = going
        left = tiles - done
        after = work(left if step == steps - 1 else -(-left * 2 // 3), after)
    advance([], [one], c, after)
    return weight_grad, hidden_grad


def solution(mesh):
    in_specs = (P("col", "row"), P("row", "col"), P("row", "col"))
    out_specs = (P("row", "col"), P("col", "row"))
    return jax.shard_map(
        functools.partial(per_device, mesh.shape["row"], mesh.shape["col"]),
        mesh=mesh, in_specs=in_specs, out_specs=out_specs, check_vma=False,
    )
```

```python
import functools

import jax
import jax.numpy as jnp
from jax import lax
from jax.experimental import pallas as pl
from jax.experimental.pallas import tpu as pltpu
from jax.sharding import PartitionSpec as P

F32, BF16 = jnp.float32, jnp.bfloat16
ANYWHERE = pl.BlockSpec(memory_space=pl.ANY)
PARAMS = pltpu.CompilerParams(vmem_limit_bytes=60 * 1024 * 1024)


def cost(flops, values):
    return pl.CostEstimate(flops=flops, bytes_accessed=2 * values, transcendentals=0)


def halving_order(bits):
    if not bits:
        return [0]
    keep = halving_order(bits[1:])
    return [o ^ bits[0] for o in keep] + keep


def flip(x, bits, n):
    return lax.ppermute(x, "col", [(i, i ^ bits[i & 1]) for i in range(n)])


def doubled(x, bits, n):
    held = {0: x}
    for bit in bits:
        pairs = [(i, i ^ bit) for i in range(n)]
        for j in list(held):
            held[j ^ bit] = lax.ppermute(held[j], "row", pairs)
    return held


def assemble_kernel(rows_of, orders, c, where_ref, *refs):
    grads_ref, turned_ref, rel = refs[-3:]
    me, row = where_ref[0], where_ref[1]
    for j, ref in zip(rows_of, refs):
        rows = ref.shape[0]
        grads_ref[pl.ds(pl.multiple_of((row ^ j) * rows, rows), rows), :] = ref[...]
    for p, (j0, j1) in enumerate(zip(*orders)):
        start = pl.multiple_of((me ^ jnp.where(me & 1, j1, j0)) * c, c)
        rel[pl.ds(p * c, c), :] = grads_ref[pl.ds(start, c), :]
    turned_ref[...] = rel[...].T


def assemble(where, blocks, orders, c, after):
    rows_of, arrays = list(blocks), list(blocks.values())
    depth, rows = arrays[0].shape[1], len(orders[0]) * c
    steps = 4
    part = pl.BlockSpec((arrays[0].shape[0], depth // steps), lambda i, s: (0, i))
    return pl.pallas_call(
        functools.partial(assemble_kernel, rows_of, orders, c),
        out_shape=(
            jax.ShapeDtypeStruct((rows, depth), BF16),
            jax.ShapeDtypeStruct((depth, rows), BF16),
        ),
        grid_spec=pltpu.PrefetchScalarGridSpec(
            num_scalar_prefetch=1,
            grid=(steps,),
            in_specs=[part] * len(arrays) + [ANYWHERE] * len(after),
            out_specs=(
                pl.BlockSpec((rows, depth // steps), lambda i, s: (0, i)),
                pl.BlockSpec((depth // steps, rows), lambda i, s: (i, 0)),
            ),
            scratch_shapes=[pltpu.VMEM((rows, depth // steps), BF16)],
        ),
        compiler_params=PARAMS,
        cost_estimate=cost(0, 3 * rows * depth),
        name="assemble",
    )(where, *arrays, *after)


def partial_kernel(w_ref, g_ref, *refs):
    send_ref, keep_ref = refs[-2:]
    res = jnp.dot(w_ref[...], g_ref[...], preferred_element_type=F32).astype(BF16).T
    rows = res.shape[0] // 2
    send_ref[...] = res[:rows].reshape(send_ref.shape)
    keep_ref[...] = res[rows:].reshape(keep_ref.shape)


def partial_sums(turned, weight, n, c, tile, first, count, after):
    depth = weight.shape[1]
    out = jax.ShapeDtypeStruct((n // 2, c, count * tile), BF16)
    out_spec = pl.BlockSpec((n // 2, c, tile), lambda i: (0, 0, i))
    return pl.pallas_call(
        partial_kernel,
        out_shape=(out, out),
        grid=(count,),
        in_specs=[
            pl.BlockSpec((tile, depth), lambda i: (first + i, 0)),
            pl.BlockSpec((depth, n * c), lambda i: (0, 0), pipeline_mode=pl.Buffered(1)),
        ]
        + [ANYWHERE] * len(after),
        out_specs=(out_spec, out_spec),
        compiler_params=PARAMS,
        cost_estimate=cost(
            2 * n * c * depth * count * tile,
            n * c * depth + count * tile * depth + n * c * count * tile,
        ),
        name="partial_sums",
    )(weight, turned, *after)


def weight_kernel(places, chunks, n, where_ref, *refs):
    acts_refs, refs = refs[: len(places)], refs[len(places):]
    grads_refs, out_ref, acts = refs[: len(chunks)], refs[-2], refs[-1]
    me = where_ref[0]
    for (j0, j1), ref in zip(places, acts_refs):
        owner = me ^ jnp.where(me & 1, j1, j0)
        for at, c in chunks:
            start = pl.multiple_of(at * n + owner * c, c)
            acts[pl.ds(start, c), :] = ref[pl.ds(at, c), :]
    total = None
    for (at, c), ref in zip(chunks, grads_refs):
        term = lax.dot_general(
            acts[pl.ds(at * n, c * n), :], ref[...],
            (((0,), (0,)), ((), ())), preferred_element_type=F32,
        )
        total = term if total is None else total + term
    out_ref[...] = total.astype(BF16)


def weight_rows(where, pieces, grads, chunks, n, before, shape, tile, first, count, after):
    places = [place for place, _ in pieces]
    rows, width = sum(g.shape[0] for g in grads), shape[1]
    in_specs = [pl.BlockSpec((a.shape[0], tile), lambda i, s: (0, first + i)) for _, a in pieces]
    in_specs += [
        pl.BlockSpec(g.shape, lambda i, s: (0, 0), pipeline_mode=pl.Buffered(1)) for g in grads
    ]
    args = [a for _, a in pieces] + list(grads) + list(after)
    in_specs += [ANYWHERE] * len(after)
    aliases = {}
    if before is not None:
        in_specs.append(ANYWHERE)
        args.append(before)
        aliases = {len(args): 0}
    return pl.pallas_call(
        functools.partial(weight_kernel, places, chunks, n),
        out_shape=jax.ShapeDtypeStruct(shape, BF16),
        grid_spec=pltpu.PrefetchScalarGridSpec(
            num_scalar_prefetch=1,
            grid=(count,),
            in_specs=in_specs,
            out_specs=pl.BlockSpec((tile, width), lambda i, s: (first + i, 0)),
            scratch_shapes=[pltpu.VMEM((rows, tile), BF16)],
        ),
        input_output_aliases=aliases,
        compiler_params=PARAMS,
        cost_estimate=cost(
            2 * rows * width * count * tile, rows * width + (rows + width) * count * tile
        ),
        name="weight_rows",
    )(where, *args)


def sums_kernel(jobs, n_final, *refs):
    n_out = len(jobs) - n_final + (n_final > 0)
    outs, base = refs[-n_out:], 0
    at = 0
    for job, (width, cuts, spans) in enumerate(jobs):
        for lo, hi in zip(cuts, cuts[1:]):
            total = None
            for (begin, end), ref in zip(spans, refs[at : at + len(spans)]):
                if begin <= lo and hi <= end:
                    term = ref[:, :, lo - begin : hi - begin].astype(F32)
                    total = term if total is None else total + term
            if job < n_out - (n_final > 0):
                outs[job][:, :, lo:hi] = total.astype(BF16)
            else:
                outs[-1][:, base + lo : base + hi] = total[0].astype(BF16)
        if job >= len(jobs) - n_final:
            base += width
        at += len(spans)


def sums(going, ended, at, shape, before, after):
    parts = going + ended
    jobs = [part.job() for part in parts]
    steps = min(2, min(part.c for part in parts) // 16)
    in_specs, args, out_specs, out_shape, values = [], [], [], [], 0
    for part, (terms, size) in zip(parts, jobs):
        for array, first, _ in terms:
            in_specs.append(
                pl.BlockSpec(
                    (size, part.c // steps, array.shape[2]),
                    lambda i, b=first // size: (b, i, 0),
                )
            )
            args.append(array)
        values += (len(terms) + 1) * size * part.c * part.width
        if part in going:
            out_specs.append(pl.BlockSpec((size, part.c // steps, part.width), lambda i: (0, i, 0)))
            out_shape.append(jax.ShapeDtypeStruct((size, part.c, part.width), BF16))
    args += after
    in_specs += [ANYWHERE] * len(after)
    aliases = {}
    if ended:
        height = ended[0].c // steps
        out_specs.append(pl.BlockSpec((height, shape[1]), lambda i: (at // height + i, 0)))
        out_shape.append(jax.ShapeDtypeStruct(shape, BF16))
        if before is not None:
            aliases = {len(args): len(going)}
            args.append(before)
            in_specs.append(ANYWHERE)
    layout = [
        (part.width, part.cuts, [span for _, _, span in terms])
        for part, (terms, _) in zip(parts, jobs)
    ]
    outs = pl.pallas_call(
        functools.partial(sums_kernel, layout, len(ended)),
        out_shape=out_shape,
        grid=(steps,),
        in_specs=in_specs,
        out_specs=out_specs,
        input_output_aliases=aliases,
        compiler_params=PARAMS,
        cost_estimate=cost(values, values),
        name="sums",
    )(*args)
    for part, out in zip(going, outs):
        part.take(out)
    return outs[-1] if ended else before, [outs[0]]


class Halving:
    def __init__(self, sends, keeps, levels, n):
        self.levels, self.n = list(levels), n
        self.half, self.c = keeps[0].shape[:2]
        self.cuts = [0]
        for keep in keeps:
            self.cuts.append(self.cuts[-1] + keep.shape[2])
        self.width = self.cuts[-1]
        spans = list(zip(self.cuts, self.cuts[1:]))
        bits = self.levels.pop(0)
        self.terms = [[keep, 0, span] for keep, span in zip(keeps, spans)]
        self.terms += [[flip(send, bits, n), 0, span] for send, span in zip(sends, spans)]

    def take(self, out):
        self.terms.append([flip(out, self.levels.pop(0), self.n), 0, (0, self.width)])

    def job(self):
        size = self.half = self.half // 2 if self.levels else 1
        job = ([tuple(term) for term in self.terms], size)
        self.terms = [[array, first + size, span] for array, first, span in self.terms]
        return job


def hold_kernel(*refs):
    refs[-1][...] = jnp.zeros_like(refs[-1])


def hold(after):
    return pl.pallas_call(
        hold_kernel,
        out_shape=jax.ShapeDtypeStruct((8, 128), F32),
        grid=(1,),
        in_specs=[ANYWHERE] * len(after),
        out_specs=pl.BlockSpec((8, 128), lambda i: (0, 0)),
        compiler_params=PARAMS,
        cost_estimate=cost(50 * 10**9, 8 * 128),
        name="hold",
    )(*after)


def per_device(n_row, n_col, hidden_acts, out_grad, down_weight):
    tokens, units = hidden_acts.shape
    features = out_grad.shape[1]
    owners = n_col // n_row
    further = [1 << b for b in range(1, n_col.bit_length() - 1)]
    levels = [(1, 1), *zip(further, further[::-1])]
    kept = [halving_order([bits[h] for bits in levels[1:]]) for h in (0, 1)]
    orders = [[o ^ 1 for o in kept[1 - h]] + kept[h] for h in (0, 1)]
    c = tokens // 2
    chunks = [(0, c), (c, c)]
    lanes = units // 128
    tile, wide = (128 * max(d for d in range(1, most + 1) if lanes % d == 0) for most in (4, 13))
    tiles = units // tile
    col, row = lax.axis_index("col"), lax.axis_index("row")
    where = jnp.stack([col, row]).astype(jnp.int32)

    whole = {bit: flip(hidden_acts, (bit, bit), n_col) for bit in further}

    by_owner = out_grad.reshape(owners, tokens, features)

    def chunk(grads, k):
        at, c = chunks[k]
        return grads[:, at : at + c].reshape(owners * c, features)

    own = [chunk(by_owner, 0)]

    row_bits = [1 << b for b in reversed(range(n_row.bit_length() - 1))]
    last = [(i, i ^ row_bits[-1]) for i in range(n_row)]

    def most(x):
        held = doubled(x, row_bits[:-1], n_row)
        return {**held, row_bits[-1]: lax.ppermute(x, "row", last)}

    def rest(held):
        more = {j ^ row_bits[-1]: a for j, a in held.items() if j not in (0, row_bits[-1])}
        return {**held, **{j: lax.ppermute(a, "row", last) for j, a in more.items()}}

    first = most(own[0])
    far, later = lax.optimization_barrier((first[row_bits[0]], by_owner))
    own.append(chunk(later, 1))
    first[row_bits[0]] = far
    first = rest(first)
    second = most(own[1])

    grads0, turned0 = assemble(where, first, orders, c, list(whole.values()))

    corners = []
    for t, bits in enumerate(levels[1:]):
        passed = [((j0 ^ bits[0], j1 ^ bits[1]), flip(a, bits, n_col)) for (j0, j1), a in corners]
        if t < len(further) - 1:
            mine = jnp.where(col & 1, whole[bits[1]], whole[bits[0]])
            corners = corners + passed + [(bits, mine)]
        else:
            corners = corners + passed
    corners = [((j0, j1), a) for (j0, j1), a in corners if j0 not in whole]

    def partials(turned, first, count, after):
        send, keep = partial_sums(turned, down_weight, n_col, c, wide, first, count, after)
        return send, keep, [send]

    count = units // wide
    cut = (count + 1) // 2
    send, keep, after = partials(turned0, 0, count, [])
    zero = Halving([send], [keep], levels, n_col)

    second, tied = lax.optimization_barrier((second, after[0]))
    arrived = [a for j, a in second.items() if j]
    second = rest(second)
    pieces = [((0, 0), hidden_acts)] + [((j, j), a) for j, a in whole.items()] + corners
    pieces += [((j1 ^ 1, j0 ^ 1), flip(a, (1, 1), n_col)) for (j0, j1), a in pieces]

    hidden_grad, weight_grad, done = None, None, 0

    def advance(going, ended, at, after):
        nonlocal hidden_grad
        hidden_grad, after = sums(going, ended, at, (tokens, units), hidden_grad, after)
        return after

    def work(count, after):
        nonlocal weight_grad, done
        count = min(tiles - done, count)
        if count:
            weight_grad = weight_rows(
                where, pieces, grads, chunks, n_col, weight_grad, (units, features), tile,
                done, count, after,
            )
            done += count
        return [weight_grad]

    after = [hold([tied] + arrived + [a for _, a in corners])]
    after = advance([zero], [], 0, after)
    exchanged = [a for _, a in pieces[n_col // 2 :]]
    grads1, turned1 = assemble(where, second, orders, c, after + exchanged[:1])
    grads = [grads0, grads1]
    sends, keeps = [], []
    for first, last in ((0, cut), (cut, count)):
        if first < last:
            send, keep, after = partials(turned1, first, last - first, after)
            sends.append(send)
            keeps.append(keep)
    one = Halving(sends, keeps, levels, n_col)
    after = work(2, after)
    parts, steps = [zero, one], len(levels) - 1
    for step in range(steps):
        going, ended = [p for p in parts if p.levels], [p for p in parts if not p.levels]
        after = advance(going, ended, 0, after)
        parts = going
        left = tiles - done
        after = work(left if step == steps - 1 else left * 9 // 11, after)
    advance([], [one], c, after)
    return weight_grad, hidden_grad


def solution(mesh):
    in_specs = (P("col", "row"), P("row", "col"), P("row", "col"))
    out_specs = (P("row", "col"), P("col", "row"))
    return jax.shard_map(
        functools.partial(per_device, mesh.shape["row"], mesh.shape["col"]),
        mesh=mesh, in_specs=in_specs, out_specs=out_specs, check_vma=False,
    )
```

```python
import functools

import jax
import jax.numpy as jnp
from jax import lax
from jax.experimental import pallas as pl
from jax.experimental.pallas import tpu as pltpu
from jax.sharding import PartitionSpec as P

F32, BF16 = jnp.float32, jnp.bfloat16
ANYWHERE = pl.BlockSpec(memory_space=pl.ANY)
PARAMS = pltpu.CompilerParams(vmem_limit_bytes=60 * 1024 * 1024)


def cost(flops, values):
    return pl.CostEstimate(flops=flops, bytes_accessed=2 * values, transcendentals=0)


def halving_order(bits):
    if not bits:
        return [0]
    keep = halving_order(bits[1:])
    return [o ^ bits[0] for o in keep] + keep


def flip(x, bits, n):
    return lax.ppermute(x, "col", [(i, i ^ bits[i & 1]) for i in range(n)])


def doubled(x, bits, n):
    held = {0: x}
    for bit in bits:
        pairs = [(i, i ^ bit) for i in range(n)]
        for j in list(held):
            held[j ^ bit] = lax.ppermute(held[j], "row", pairs)
    return held


def assemble_kernel(rows_of, orders, c, where_ref, *refs):
    grads_ref, turned_ref, rel = refs[-3:]
    me, row = where_ref[0], where_ref[1]
    for j, ref in zip(rows_of, refs):
        rows = ref.shape[0]
        grads_ref[pl.ds(pl.multiple_of((row ^ j) * rows, rows), rows), :] = ref[...]
    for p, (j0, j1) in enumerate(zip(*orders)):
        start = pl.multiple_of((me ^ jnp.where(me & 1, j1, j0)) * c, c)
        rel[pl.ds(p * c, c), :] = grads_ref[pl.ds(start, c), :]
    turned_ref[...] = rel[...].T


def assemble(where, blocks, orders, c, after):
    rows_of, arrays = list(blocks), list(blocks.values())
    depth, rows = arrays[0].shape[1], len(orders[0]) * c
    steps = 2
    part = pl.BlockSpec((arrays[0].shape[0], depth // steps), lambda i, s: (0, i))
    return pl.pallas_call(
        functools.partial(assemble_kernel, rows_of, orders, c),
        out_shape=(
            jax.ShapeDtypeStruct((rows, depth), BF16),
            jax.ShapeDtypeStruct((depth, rows), BF16),
        ),
        grid_spec=pltpu.PrefetchScalarGridSpec(
            num_scalar_prefetch=1,
            grid=(steps,),
            in_specs=[part] * len(arrays) + [ANYWHERE] * len(after),
            out_specs=(
                pl.BlockSpec((rows, depth // steps), lambda i, s: (0, i)),
                pl.BlockSpec((depth // steps, rows), lambda i, s: (i, 0)),
            ),
            scratch_shapes=[pltpu.VMEM((rows, depth // steps), BF16)],
        ),
        compiler_params=PARAMS,
        cost_estimate=cost(0, 3 * rows * depth),
        name="assemble",
    )(where, *arrays, *after)


def partial_kernel(w_ref, g_ref, *refs):
    send_ref, keep_ref = refs[-2:]
    res = jnp.dot(w_ref[...], g_ref[...], preferred_element_type=F32).astype(BF16).T
    rows = res.shape[0] // 2
    send_ref[...] = res[:rows].reshape(send_ref.shape)
    keep_ref[...] = res[rows:].reshape(keep_ref.shape)


def partial_sums(turned, weight, n, c, tile, first, count, after):
    depth = weight.shape[1]
    out = jax.ShapeDtypeStruct((n // 2, c, count * tile), BF16)
    out_spec = pl.BlockSpec((n // 2, c, tile), lambda i: (0, 0, i))
    return pl.pallas_call(
        partial_kernel,
        out_shape=(out, out),
        grid=(count,),
        in_specs=[
            pl.BlockSpec((tile, depth), lambda i: (first + i, 0)),
            pl.BlockSpec((depth, n * c), lambda i: (0, 0), pipeline_mode=pl.Buffered(1)),
        ]
        + [ANYWHERE] * len(after),
        out_specs=(out_spec, out_spec),
        compiler_params=PARAMS,
        cost_estimate=cost(
            2 * n * c * depth * count * tile,
            n * c * depth + count * tile * depth + n * c * count * tile,
        ),
        name="partial_sums",
    )(weight, turned, *after)


def weight_kernel(places, chunks, n, where_ref, *refs):
    acts_refs, refs = refs[: len(places)], refs[len(places):]
    grads_refs, out_ref, acts = refs[: len(chunks)], refs[-2], refs[-1]
    me = where_ref[0]
    for (j0, j1), ref in zip(places, acts_refs):
        owner = me ^ jnp.where(me & 1, j1, j0)
        for at, c in chunks:
            start = pl.multiple_of(at * n + owner * c, c)
            acts[pl.ds(start, c), :] = ref[pl.ds(at, c), :]
    total = None
    for (at, c), ref in zip(chunks, grads_refs):
        term = lax.dot_general(
            acts[pl.ds(at * n, c * n), :], ref[...],
            (((0,), (0,)), ((), ())), preferred_element_type=F32,
        )
        total = term if total is None else total + term
    out_ref[...] = total.astype(BF16)


def weight_rows(where, pieces, grads, chunks, n, before, shape, tile, first, count, after):
    places = [place for place, _ in pieces]
    rows, width = sum(g.shape[0] for g in grads), shape[1]
    in_specs = [pl.BlockSpec((a.shape[0], tile), lambda i, s: (0, first + i)) for _, a in pieces]
    in_specs += [
        pl.BlockSpec(g.shape, lambda i, s: (0, 0), pipeline_mode=pl.Buffered(1)) for g in grads
    ]
    args = [a for _, a in pieces] + list(grads) + list(after)
    in_specs += [ANYWHERE] * len(after)
    aliases = {}
    if before is not None:
        in_specs.append(ANYWHERE)
        args.append(before)
        aliases = {len(args): 0}
    return pl.pallas_call(
        functools.partial(weight_kernel, places, chunks, n),
        out_shape=jax.ShapeDtypeStruct(shape, BF16),
        grid_spec=pltpu.PrefetchScalarGridSpec(
            num_scalar_prefetch=1,
            grid=(count,),
            in_specs=in_specs,
            out_specs=pl.BlockSpec((tile, width), lambda i, s: (first + i, 0)),
            scratch_shapes=[pltpu.VMEM((rows, tile), BF16)],
        ),
        input_output_aliases=aliases,
        compiler_params=PARAMS,
        cost_estimate=cost(
            2 * rows * width * count * tile, rows * width + (rows + width) * count * tile
        ),
        name="weight_rows",
    )(where, *args)


def sums_kernel(jobs, n_final, *refs):
    n_out = len(jobs) - n_final + (n_final > 0)
    outs, base = refs[-n_out:], 0
    at = 0
    for job, (width, cuts, spans) in enumerate(jobs):
        for lo, hi in zip(cuts, cuts[1:]):
            total = None
            for (begin, end), ref in zip(spans, refs[at : at + len(spans)]):
                if begin <= lo and hi <= end:
                    term = ref[:, :, lo - begin : hi - begin].astype(F32)
                    total = term if total is None else total + term
            if job < n_out - (n_final > 0):
                outs[job][:, :, lo:hi] = total.astype(BF16)
            else:
                outs[-1][:, base + lo : base + hi] = total[0].astype(BF16)
        if job >= len(jobs) - n_final:
            base += width
        at += len(spans)


def sums(going, ended, at, shape, before, after):
    parts = going + ended
    jobs = [part.job() for part in parts]
    steps = min(2, min(part.c for part in parts) // 16)
    in_specs, args, out_specs, out_shape, values = [], [], [], [], 0
    for part, (terms, size) in zip(parts, jobs):
        for array, first, _ in terms:
            in_specs.append(
                pl.BlockSpec(
                    (size, part.c // steps, array.shape[2]),
                    lambda i, b=first // size: (b, i, 0),
                )
            )
            args.append(array)
        values += (len(terms) + 1) * size * part.c * part.width
        if part in going:
            out_specs.append(pl.BlockSpec((size, part.c // steps, part.width), lambda i: (0, i, 0)))
            out_shape.append(jax.ShapeDtypeStruct((size, part.c, part.width), BF16))
    args += after
    in_specs += [ANYWHERE] * len(after)
    aliases = {}
    if ended:
        height = ended[0].c // steps
        out_specs.append(pl.BlockSpec((height, shape[1]), lambda i: (at // height + i, 0)))
        out_shape.append(jax.ShapeDtypeStruct(shape, BF16))
        if before is not None:
            aliases = {len(args): len(going)}
            args.append(before)
            in_specs.append(ANYWHERE)
    layout = [
        (part.width, part.cuts, [span for _, _, span in terms])
        for part, (terms, _) in zip(parts, jobs)
    ]
    outs = pl.pallas_call(
        functools.partial(sums_kernel, layout, len(ended)),
        out_shape=out_shape,
        grid=(steps,),
        in_specs=in_specs,
        out_specs=out_specs,
        input_output_aliases=aliases,
        compiler_params=PARAMS,
        cost_estimate=cost(values, values),
        name="sums",
    )(*args)
    for part, out in zip(going, outs):
        part.take(out)
    return outs[-1] if ended else before, [outs[0]]


class Halving:
    def __init__(self, sends, keeps, levels, n):
        self.levels, self.n = list(levels), n
        self.half, self.c = keeps[0].shape[:2]
        self.cuts = [0]
        for keep in keeps:
            self.cuts.append(self.cuts[-1] + keep.shape[2])
        self.width = self.cuts[-1]
        spans = list(zip(self.cuts, self.cuts[1:]))
        bits = self.levels.pop(0)
        self.terms = [[keep, 0, span] for keep, span in zip(keeps, spans)]
        self.terms += [[flip(send, bits, n), 0, span] for send, span in zip(sends, spans)]

    def take(self, out):
        self.terms.append([flip(out, self.levels.pop(0), self.n), 0, (0, self.width)])

    def job(self):
        size = self.half = self.half // 2 if self.levels else 1
        job = ([tuple(term) for term in self.terms], size)
        self.terms = [[array, first + size, span] for array, first, span in self.terms]
        return job


def hold_kernel(*refs):
    refs[-1][...] = jnp.zeros_like(refs[-1])


def hold(after):
    return pl.pallas_call(
        hold_kernel,
        out_shape=jax.ShapeDtypeStruct((8, 128), F32),
        grid=(1,),
        in_specs=[ANYWHERE] * len(after),
        out_specs=pl.BlockSpec((8, 128), lambda i: (0, 0)),
        compiler_params=PARAMS,
        cost_estimate=cost(50 * 10**9, 8 * 128),
        name="hold",
    )(*after)


def per_device(n_row, n_col, hidden_acts, out_grad, down_weight):
    tokens, units = hidden_acts.shape
    features = out_grad.shape[1]
    owners = n_col // n_row
    further = [1 << b for b in range(1, n_col.bit_length() - 1)]
    levels = [(1, 1), *zip(further, further[::-1])]
    kept = [halving_order([bits[h] for bits in levels[1:]]) for h in (0, 1)]
    orders = [[o ^ 1 for o in kept[1 - h]] + kept[h] for h in (0, 1)]
    c = tokens // 2
    chunks = [(0, c), (c, c)]
    lanes = units // 128
    tile, wide = (128 * max(d for d in range(1, most + 1) if lanes % d == 0) for most in (4, 13))
    tiles = units // tile
    col, row = lax.axis_index("col"), lax.axis_index("row")
    where = jnp.stack([col, row]).astype(jnp.int32)

    whole = {bit: flip(hidden_acts, (bit, bit), n_col) for bit in further}

    by_owner = out_grad.reshape(owners, tokens, features)

    def chunk(grads, k):
        at, c = chunks[k]
        return grads[:, at : at + c].reshape(owners * c, features)

    own = [chunk(by_owner, 0)]

    row_bits = [1 << b for b in reversed(range(n_row.bit_length() - 1))]
    last = [(i, i ^ row_bits[-1]) for i in range(n_row)]

    def most(x):
        held = doubled(x, row_bits[:-1], n_row)
        return {**held, row_bits[-1]: lax.ppermute(x, "row", last)}

    def rest(held):
        more = {j ^ row_bits[-1]: a for j, a in held.items() if j not in (0, row_bits[-1])}
        return {**held, **{j: lax.ppermute(a, "row", last) for j, a in more.items()}}

    first = most(own[0])
    far, later = lax.optimization_barrier((first[row_bits[0]], by_owner))
    own.append(chunk(later, 1))
    first[row_bits[0]] = far
    first = rest(first)
    second = most(own[1])

    grads0, turned0 = assemble(where, first, orders, c, list(whole.values()))

    corners = []
    for t, bits in enumerate(levels[1:]):
        passed = [((j0 ^ bits[0], j1 ^ bits[1]), flip(a, bits, n_col)) for (j0, j1), a in corners]
        if t < len(further) - 1:
            mine = jnp.where(col & 1, whole[bits[1]], whole[bits[0]])
            corners = corners + passed + [(bits, mine)]
        else:
            corners = corners + passed
    corners = [((j0, j1), a) for (j0, j1), a in corners if j0 not in whole]

    def partials(turned, first, count, after):
        send, keep = partial_sums(turned, down_weight, n_col, c, wide, first, count, after)
        return send, keep, [send]

    count = units // wide
    cut = (count + 1) // 2
    send, keep, after = partials(turned0, 0, count, [])
    zero = Halving([send], [keep], levels, n_col)

    second, tied = lax.optimization_barrier((second, after[0]))
    arrived = [a for j, a in second.items() if j]
    second = rest(second)
    pieces = [((0, 0), hidden_acts)] + [((j, j), a) for j, a in whole.items()] + corners
    pieces += [((j1 ^ 1, j0 ^ 1), flip(a, (1, 1), n_col)) for (j0, j1), a in pieces]

    hidden_grad, weight_grad, done = None, None, 0

    def advance(going, ended, at, after):
        nonlocal hidden_grad
        hidden_grad, after = sums(going, ended, at, (tokens, units), hidden_grad, after)
        return after

    def work(count, after):
        nonlocal weight_grad, done
        count = min(tiles - done, count)
        if count:
            weight_grad = weight_rows(
                where, pieces, grads, chunks, n_col, weight_grad, (units, features), tile,
                done, count, after,
            )
            done += count
        return [weight_grad]

    after = [hold([tied] + arrived + [a for _, a in corners])]
    after = advance([zero], [], 0, after)
    exchanged = [a for _, a in pieces[n_col // 2 :]]
    grads1, turned1 = assemble(where, second, orders, c, after + exchanged[:1])
    grads = [grads0, grads1]
    sends, keeps = [], []
    for first, last in ((0, cut), (cut, count)):
        if first < last:
            send, keep, after = partials(turned1, first, last - first, after)
            sends.append(send)
            keeps.append(keep)
    one = Halving(sends, keeps, levels, n_col)
    after = work(2, after)
    parts, steps = [zero, one], len(levels) - 1
    for step in range(steps):
        going, ended = [p for p in parts if p.levels], [p for p in parts if not p.levels]
        after = advance(going, ended, 0, after)
        parts = going
        left = tiles - done
        after = work(left if step == steps - 1 else left * 9 // 11, after)
    advance([], [one], c, after)
    return weight_grad, hidden_grad


def solution(mesh):
    in_specs = (P("col", "row"), P("row", "col"), P("row", "col"))
    out_specs = (P("row", "col"), P("col", "row"))
    return jax.shard_map(
        functools.partial(per_device, mesh.shape["row"], mesh.shape["col"]),
        mesh=mesh, in_specs=in_specs, out_specs=out_specs, check_vma=False,
    )
```
